512 devices in a mesh: mem: 8 (over y_hi, x), lon: 64 (over z, y_lo, core).
Axes of the slice: x: 4, y: 8 (y_hi: 2, y_lo: 4; y = y_hi * 4 + y_lo), z: 8, core: 2. Of those that a mesh axis runs over, the one named last changes fastest.
Arguments:
- control: bfloat16 [16, 64, 512, 512], P('mem', None, 'lon'), may hold values from -6 to 6
- perturb: bfloat16 [16, 64, 512, 512], P('mem', None, 'lon'), may hold values from -1.5 to 1.5
- member_group: int32 [16], P('mem'), may hold values from 0 to 3, as said below
- group_weight: float32 [4], replicated, may hold values from 0.25 to 4
- step_counts: int32 [64], replicated, may hold values from 1 to 4, as said below
- lat_inverse: bfloat16 [512, 512], replicated, may hold values from -0.25 to 0.25
- vert_inverse: float32 [64, 64], replicated, may hold values from -0.75 to 0.75
- innovation: bfloat16 [64, 512, 512], P(None, 'lon'), may hold values from -6 to 6
- precision: bfloat16 [64, 512, 512], P(None, 'lon'), may hold values from 2 to 20
Outputs:
- gradient: bfloat16 [16, 64, 512, 512], P('mem', None, 'lon')
The draws below stay inside these ranges and needn't reach their ends.
Inputs may be any that keep to these rules, and one draw needn't show every extreme that they name: `step_counts`: some level takes 4 steps and some level takes 1. `member_group`: some member belongs to group 0 and some member to group 4 - 1.
All inputs are finite; a program needn't handle non-finite values.
Results may differ from the reference program's by a relative error of at most 0.013.
Values may be sent and summed in bfloat16 or wider, within the bound.
No kernel may reach another device: no remote copies, remote signals or barrier semaphores. Data moves between devices by JAX's collectives and lax.ppermute only.
A program may use at most 64 MiB of HBM per device.

```python
import math
import jax
import jax.numpy as jnp
from jax import lax

LEV = 64
LAT = 512
KMAX = 4
NG = 4
M = 16
LON = 512


def draw_step_counts(key, part):
    key = jax.random.fold_in(key, 7)
    key_counts, key_high, key_low = jax.random.split(key, 3)
    counts = jax.random.randint(key_counts, (LEV,), 1, KMAX + 1)
    highest = jax.random.randint(key_high, (), 0, LEV)
    spacing = jax.random.randint(key_low, (), 1, LEV)
    lowest = (highest + spacing) % LEV
    positions = jnp.arange(LEV)
    counts = jnp.where(positions == highest, KMAX, counts)
    counts = jnp.where(positions == lowest, 1, counts)
    return counts.astype(jnp.int32)


def draw_member_group(key, part):
    key = jax.random.fold_in(key, 11)
    key_groups, key_first, key_second = jax.random.split(key, 3)
    groups = jax.random.randint(key_groups, (M,), 0, NG)
    first = jax.random.randint(key_first, (), 0, M)
    spacing = jax.random.randint(key_second, (), 1, M)
    second = (first + spacing) % M
    positions = jnp.arange(M)
    groups = jnp.where(positions == first, 0, groups)
    groups = jnp.where(positions == second, NG - 1, groups)
    return groups.astype(jnp.int32)


def block_scale(own_key, shape, cuts, low, top_value):
    loudness = 1.0
    for axis_at, blocks in cuts:
        steps = jax.random.uniform(jax.random.fold_in(jax.random.fold_in(own_key, 6), axis_at), (blocks,), jnp.float32, low / len(cuts), top_value / len(cuts))
        loudness = loudness * jnp.repeat(jnp.exp(steps), shape[axis_at] // blocks).reshape((-1,) + (1,) * (len(shape) - 1 - axis_at))
    return loudness


def bell_draw(stream_key, dims, scale, reach, cuts=(), held_as=jnp.bfloat16):
    drawn = jax.random.normal(stream_key, dims, jnp.float32) * scale
    if len(cuts) > 0:
        drawn = block_scale(stream_key, dims, cuts, -0.22, 0.18) * drawn
    return jnp.clip(drawn, min=-reach, max=reach).astype(held_as)


def setup_inputs(seed: int = 0) -> dict:
    key_of = jax.random.split(jax.random.key(seed), 10)
    control = bell_draw(key_of[0], (M, LEV, LON, LAT), 1.0, 6.0, ((0, 8), (2, 64)))
    perturb = bell_draw(key_of[1], (M, LEV, LON, LAT), M ** -0.5, 1.5, ((0, 8), (2, 64)))
    member_group = draw_member_group(jax.random.fold_in(key_of[9], 71), 0)
    group_weight = jnp.clip(jnp.exp(jax.random.uniform(key_of[3], (NG,), jnp.float32, math.log(0.25), math.log(4.0))), 0.25, 4.0)
    step_counts = draw_step_counts(jax.random.fold_in(key_of[9], 71), 0)
    lat_inverse = bell_draw(key_of[5], (LAT, LAT), LAT ** -0.5, 0.25)
    vert_inverse = bell_draw(key_of[6], (LEV, LEV), LEV ** -0.5, 0.75, (), jnp.float32)
    innovation = bell_draw(key_of[7], (LEV, LON, LAT), 1.0, 6.0, ((1, 64),))
    precision = jnp.clip(jnp.exp(math.log(20.0) - 2.3025851 * jax.random.uniform(key_of[8], (LEV, LON, LAT), jnp.float32) ** block_scale(key_of[8], (LEV, LON, LAT), ((1, 64),), -0.2, 0.2)), 2.0, 20.0).astype(jnp.bfloat16)
    return dict(control=control, perturb=perturb, member_group=member_group, group_weight=group_weight, step_counts=step_counts, lat_inverse=lat_inverse, vert_inverse=vert_inverse, innovation=innovation, precision=precision)


diffusion_number = 0.5


def diffuse(values, step_counts):
    for sweep in range(KMAX):
        active = (step_counts > sweep)[:, None, None]
        left = jnp.roll(values, 1, axis=1)
        right = jnp.roll(values, -1, axis=1)
        second = left + right - 2.0 * values
        values = values + jnp.where(active, diffusion_number * second, jnp.float32(0.0))
    return values


def reference(control, perturb, member_group, group_weight, step_counts, lat_inverse, vert_inverse, innovation, precision):
    member_weight = group_weight[member_group]

    def forward(running, inputs):
        member_control, member_perturb, weight_one = inputs
        spread = diffuse(member_control.astype(jnp.float32), step_counts).astype(jnp.bfloat16)
        latmix = jnp.dot(spread, lat_inverse, preferred_element_type=jnp.float32)
        local_part = jnp.einsum("kl,lxy->kxy", vert_inverse, latmix, precision=lax.Precision.HIGHEST)
        return running + weight_one * member_perturb.astype(jnp.float32) * local_part, None

    start_zero = jnp.zeros(innovation.shape, jnp.float32)
    increment, unused = lax.scan(forward, start_zero, (control, perturb, member_weight))
    misfit = (precision.astype(jnp.float32) * (increment - innovation.astype(jnp.float32))).astype(jnp.bfloat16)

    def adjoint(inputs):
        member_control, member_perturb, weight_one = inputs
        back = weight_one * member_perturb.astype(jnp.float32) * misfit.astype(jnp.float32)
        vertback = jnp.einsum("kl,kxy->lxy", vert_inverse, back, precision=lax.Precision.HIGHEST).astype(jnp.bfloat16)
        latback = lax.dot_general(vertback, lat_inverse, (((2,), (1,)), ((), ())), preferred_element_type=jnp.float32)
        return (member_control.astype(jnp.float32) + diffuse(latback, step_counts)).astype(jnp.bfloat16)

    return lax.map(adjoint, (control, perturb, member_weight))
```

```python
import functools

import jax
import jax.numpy as jnp
from jax import lax
from jax.experimental import pallas as pl
from jax.experimental.pallas import tpu as pltpu
from jax.sharding import PartitionSpec as P

LEV = 64
ROWS = 8
LAT = 512
KMAX = 4
HALO = 4
MEMBERS = 2
XS = 4
OWN = LEV * ROWS
SIDE = LEV * HALO

BF = jnp.bfloat16
F32 = jnp.float32
VMEM = pl.BlockSpec(memory_space=pltpu.VMEM)
SMEM = pl.BlockSpec(memory_space=pltpu.SMEM)

BAND = {
    1: {1: 0.5},
    2: {0: 0.5, 2: 0.25},
    3: {1: 0.375, 3: 0.125},
    4: {0: 0.375, 2: 0.25, 4: 0.0625},
}


def call(kernel, out, operands, specs, flops, moved):
    return pl.pallas_call(
        kernel,
        out_shape=out,
        in_specs=specs,
        out_specs=jax.tree.map(lambda _: VMEM, out),
        compiler_params=pltpu.CompilerParams(vmem_limit_bytes=40 * 2**20),
        cost_estimate=pl.CostEstimate(flops=flops, bytes_accessed=moved, transcendentals=0),
    )(*operands)


def halves(x):
    columns = x.shape[1]
    x = x.reshape(LEV // 2, 2, ROWS, columns)
    even, odd = x[:, 0], x[:, 1]
    low = lax.broadcasted_iota(jnp.int32, even.shape, 1) < HALO
    top = jnp.where(low, even, pltpu.roll(odd, HALO, 1))
    bottom = jnp.where(low, pltpu.roll(even, HALO, 1), odd)
    return top.reshape(SIDE, columns), bottom.reshape(SIDE, columns)


def pack_kernel(x_ref, top_ref, bottom_ref):
    for m in range(x_ref.shape[0]):
        top, bottom = halves(x_ref[m].astype(F32))
        top_ref[m] = top.astype(BF)
        bottom_ref[m] = bottom.astype(BF)


def pack(x):
    members = x.shape[0]
    half = jax.ShapeDtypeStruct((members, SIDE, LAT), BF)
    return call(pack_kernel, (half, half), (x,), [VMEM], 0, 4 * members * OWN * LAT)


def weights(n, distance):
    total = jnp.zeros(distance.shape, F32)
    for sweeps, band in BAND.items():
        row = jnp.zeros(distance.shape, F32)
        for d, c in band.items():
            row = jnp.where(jnp.abs(distance) == d, jnp.float32(c), row)
        total = jnp.where(n == sweeps, row, total)
    return total


def spread_lanes(width, per):
    level = lax.broadcasted_iota(jnp.int32, (LEV, width), 0)
    lane = lax.broadcasted_iota(jnp.int32, (LEV, width), 1)
    return jnp.where(level == lane // per, F32(1.0), F32(0.0)).astype(BF)


def side_distance():
    row = lax.broadcasted_iota(jnp.int32, (ROWS, 2 * SIDE), 0)
    lane = lax.broadcasted_iota(jnp.int32, (ROWS, 2 * SIDE), 1)
    place = jnp.where(lane < SIDE, lane % HALO - HALO, lane % HALO + ROWS)
    return place - row


def own_distance():
    row = lax.broadcasted_iota(jnp.int32, (ROWS, OWN), 0)
    lane = lax.broadcasted_iota(jnp.int32, (ROWS, OWN), 1)
    return lane % ROWS - row


def first_kernel(
    group_ref, weight_ref, steps_ref, steps_row_ref, vert_ref, lat_ref, control_ref, perturb_ref,
    side_ref, back_own_ref, back_side_ref, partial_ref, table,
):
    vert = vert_ref[...].astype(BF)
    steps_row = steps_row_ref[...].astype(F32).astype(BF)
    lanes_own = spread_lanes(OWN, ROWS)
    lanes_half = spread_lanes(SIDE, HALO)
    lanes_side = jnp.concatenate([lanes_half, lanes_half], axis=1)

    def expand(matrix, lanes, dims=(((1,), (0,)), ((), ()))):
        return lax.dot_general(matrix, lanes, dims, preferred_element_type=F32)

    def forward(lanes, distance):
        n = expand(steps_row, lanes)
        wide = expand(vert, lanes)
        band = weights(n, distance)
        return (wide[:, None, :] * band[None]).reshape(OWN, OWN).astype(BF)

    side_ref[...] = forward(lanes_side, side_distance())
    own = forward(lanes_own, own_distance())

    first_dim = (((0,), (0,)), ((), ()))
    for lanes, distance, out_ref in (
        (lanes_own, own_distance(), back_own_ref),
        (lanes_side, side_distance(), back_side_ref),
    ):
        wide = expand(vert, lanes, first_dim)
        for n in range(1, KMAX + 1):
            table[n - 1] = weights(n, distance)
        for l in range(0, LEV, 2):
            pair = [wide[l + i : l + i + 1] * table[steps_ref[l + i] - 1] for i in range(2)]
            out_ref[pl.ds(l * ROWS, 2 * ROWS), :] = jnp.concatenate(pair, axis=0).astype(BF)

    total = jnp.zeros((OWN, LAT), F32)
    for m in range(MEMBERS):
        mixed = jnp.dot(own, control_ref[m], preferred_element_type=F32).astype(BF)
        local = jnp.dot(mixed, lat_ref[...], preferred_element_type=F32)
        weight = weight_ref[group_ref[m]]
        total = total + (weight * perturb_ref[m].astype(F32)) * local
    partial_ref[...] = total


def forward_kernel(
    group_ref, weight_ref, side_ref, lat_ref, left_ref, right_ref, perturb_ref, partial_ref, out_ref
):
    total = partial_ref[...]
    for m in range(MEMBERS):
        mixed = jnp.dot(side_ref[:, :SIDE], left_ref[m], preferred_element_type=F32)
        mixed += jnp.dot(side_ref[:, SIDE:], right_ref[m], preferred_element_type=F32)
        local = jnp.dot(mixed.astype(BF), lat_ref[...], preferred_element_type=F32)
        weight = weight_ref[group_ref[m]]
        total = total + (weight * perturb_ref[m].astype(F32)) * local
    out_ref[...] = total.astype(BF)


LAST = (((1,), (1,)), ((), ()))


def back_own_kernel(
    group_ref, weight_ref, back_own_ref, lat_ref, misfit_ref, perturb_ref, control_ref, out_ref
):
    misfit = misfit_ref[...].astype(F32)
    for m in range(MEMBERS):
        weight = weight_ref[group_ref[m]]
        back = ((weight * perturb_ref[m].astype(F32)) * misfit).astype(BF)
        mixed = jnp.dot(back_own_ref[...], back, preferred_element_type=F32).astype(BF)
        latback = lax.dot_general(mixed, lat_ref[...], LAST, preferred_element_type=F32)
        out_ref[m] = control_ref[m].astype(F32) + latback


def back_side_kernel(
    group_ref, weight_ref, back_side_ref, lat_ref, left_ref, right_ref, p_left_ref, p_right_ref,
    base_ref, out_ref,
):
    left = left_ref[...].astype(F32)
    right = right_ref[...].astype(F32)
    for m in range(MEMBERS):
        weight = weight_ref[group_ref[m]]
        from_left = ((weight * p_left_ref[m].astype(F32)) * left).astype(BF)
        from_right = ((weight * p_right_ref[m].astype(F32)) * right).astype(BF)
        mixed = jnp.dot(back_side_ref[:, :SIDE], from_left, preferred_element_type=F32)
        mixed += jnp.dot(back_side_ref[:, SIDE:], from_right, preferred_element_type=F32)
        latback = lax.dot_general(mixed.astype(BF), lat_ref[...], LAST, preferred_element_type=F32)
        out_ref[m] = (base_ref[m] + latback).astype(BF)


def shards(
    control,
    perturb,
    member_group,
    group_weight,
    step_counts,
    lat_inverse,
    vert_inverse,
    innovation,
    precision,
):
    lons = lax.axis_size("lon")
    up = [(i, (i + 1) % lons) for i in range(lons)]
    down = [(j, i) for i, j in up]
    mems = lax.axis_size("mem")
    along_x = [list(range(i, i + XS)) for i in range(0, mems, XS)]
    across_y = [(i, (i + XS) % mems) for i in range(mems)]
    x = lax.axis_index("mem") % XS

    def halo(top, bottom):
        return lax.ppermute(bottom, "lon", up), lax.ppermute(top, "lon", down)

    control = control.reshape(MEMBERS, OWN, LAT)
    perturb = perturb.reshape(MEMBERS, OWN, LAT)
    c_left, c_right = halo(*pack(control))
    p_left, p_right = halo(*pack(perturb))

    square = OWN * LAT
    matmul = 2 * OWN * LAT * LAT
    side, back_own, back_side, partial = call(
        first_kernel_with_table,
        (
            jax.ShapeDtypeStruct((OWN, 2 * SIDE), BF),
            jax.ShapeDtypeStruct((OWN, OWN), BF),
            jax.ShapeDtypeStruct((OWN, 2 * SIDE), BF),
            jax.ShapeDtypeStruct((OWN, LAT), F32),
        ),
        (member_group, group_weight, step_counts, step_counts.reshape(1, LEV), vert_inverse,
         lat_inverse, control, perturb),
        [SMEM, SMEM, SMEM] + [VMEM] * 5,
        4 * matmul, 20 * square,
    )
    partial = call(
        forward_kernel,
        jax.ShapeDtypeStruct((OWN, LAT), BF),
        (member_group, group_weight, side, lat_inverse, c_left, c_right, perturb, partial),
        [SMEM, SMEM] + [VMEM] * 6,
        4 * matmul, 18 * square,
    )

    quarter = OWN // XS
    parts = lax.all_to_all(
        partial.reshape(XS, quarter, LAT), "mem", 0, 0, axis_index_groups=along_x
    )
    some = jnp.sum(parts.astype(F32), axis=0).astype(BF)
    other = lax.ppermute(some, "mem", across_y)
    increment = some.astype(F32) + other.astype(F32)
    innov = lax.dynamic_slice_in_dim(innovation.reshape(OWN, LAT), x * quarter, quarter, 0)
    prec = lax.dynamic_slice_in_dim(precision.reshape(OWN, LAT), x * quarter, quarter, 0)
    misfit = (prec.astype(F32) * (increment - innov.astype(F32))).astype(BF)
    misfit = lax.all_to_all(
        jnp.broadcast_to(misfit, (XS, quarter, LAT)), "mem", 0, 0, axis_index_groups=along_x
    ).reshape(OWN, LAT)

    top, bottom = pack(misfit[None])
    m_left, m_right = halo(top[0], bottom[0])
    base = call(
        back_own_kernel,
        jax.ShapeDtypeStruct((MEMBERS, OWN, LAT), F32),
        (member_group, group_weight, back_own, lat_inverse, misfit, perturb, control),
        [SMEM, SMEM] + [VMEM] * 5,
        4 * matmul, 18 * square,
    )
    out = call(
        back_side_kernel,
        jax.ShapeDtypeStruct((MEMBERS, OWN, LAT), BF),
        (member_group, group_weight, back_side, lat_inverse, m_left, m_right, p_left, p_right, base),
        [SMEM, SMEM] + [VMEM] * 7,
        4 * matmul, 20 * square,
    )
    return out.reshape(MEMBERS, LEV, ROWS, LAT)


def first_kernel_with_table(*refs):
    pl.run_scoped(
        functools.partial(first_kernel, *refs), pltpu.VMEM((KMAX, ROWS, OWN), F32)
    )


def solution(mesh):
    return jax.shard_map(
        shards,
        mesh=mesh,
        in_specs=(
            P("mem", None, "lon", None),
            P("mem", None, "lon", None),
            P("mem"),
            P(),
            P(),
            P(),
            P(),
            P(None, "lon", None),
            P(None, "lon", None),
        ),
        out_specs=P("mem", None, "lon", None),
        check_vma=False,
    )
```

```python
import jax
import jax.numpy as jnp
from jax import lax
from jax.experimental import pallas as pl
from jax.experimental.pallas import tpu as pltpu
from jax.sharding import PartitionSpec as P

LEV = 64
ROWS = 8
LAT = 512
KMAX = 4
HALO = 4
MEMBERS = 2
XS = 4
PACK_PARTS = 4
OWN = LEV * ROWS
SIDE = LEV * HALO

VMEM_LIMIT = 16 * 2**20

BF = jnp.bfloat16
F32 = jnp.float32
VMEM = pl.BlockSpec(memory_space=pltpu.VMEM)
HBM = pl.BlockSpec(memory_space=pltpu.HBM)

BAND = {
    1: {1: 0.5},
    2: {0: 0.5, 2: 0.25},
    3: {1: 0.375, 3: 0.125},
    4: {0: 0.375, 2: 0.25, 4: 0.0625},
}


def in_hbm(x):
    return pltpu.with_memory_space_constraint(x, pltpu.HBM)


def call(kernel, out, operands, specs, flops, moved, scratch=()):
    return pl.pallas_call(
        kernel,
        out_shape=out,
        in_specs=specs,
        out_specs=jax.tree.map(lambda _: VMEM, out),
        scratch_shapes=scratch,
        compiler_params=pltpu.CompilerParams(vmem_limit_bytes=VMEM_LIMIT),
        cost_estimate=pl.CostEstimate(flops=flops, bytes_accessed=moved, transcendentals=0),
    )(*(in_hbm(x) if spec is HBM else x for x, spec in zip(operands, specs)))


def halves(x):
    rows, columns = x.shape
    x = x.reshape(rows // (2 * ROWS), 2, ROWS, columns)
    even, odd = x[:, 0], x[:, 1]
    low = lax.broadcasted_iota(jnp.int32, even.shape, 1) < HALO
    top = jnp.where(low, even, pltpu.roll(odd, HALO, 1))
    bottom = jnp.where(low, pltpu.roll(even, HALO, 1), odd)
    return top.reshape(rows // 2, columns), bottom.reshape(rows // 2, columns)


def odd_place():
    return lax.rem(lax.axis_index("lon"), 2) == 1


def pack_into(odd, x, outer_ref, inner_ref, at):
    top, bottom = halves(x.astype(F32))
    outer_ref[at] = jnp.where(odd, bottom, top).astype(BF)
    inner_ref[at] = jnp.where(odd, top, bottom).astype(BF)


def pack_kernel(x_ref, outer_ref, inner_ref, x, sems):
    odd = odd_place()
    part = OWN // PACK_PARTS
    copies = []
    for i in range(MEMBERS * PACK_PARTS):
        rows = (i // PACK_PARTS, pl.ds(i % PACK_PARTS * part, part))
        copies.append(pltpu.make_async_copy(x_ref.at[rows], x.at[rows], sems.at[i]))
        copies[-1].start()
    for i, copy in enumerate(copies):
        copy.wait()
        m, p = i // PACK_PARTS, i % PACK_PARTS
        pack_into(odd, x[m, pl.ds(p * part, part)], outer_ref, inner_ref, (m, pl.ds(p * part // 2, part // 2)))


def half_like(members):
    return jax.ShapeDtypeStruct((members, SIDE, LAT), BF)


def weights(n, distance):
    total = jnp.zeros(distance.shape, F32)
    for sweeps, band in BAND.items():
        row = jnp.zeros(distance.shape, F32)
        for d, c in band.items():
            row = jnp.where(jnp.abs(distance) == d, jnp.float32(c), row)
        total = jnp.where(n == sweeps, row, total)
    return total


def spread_lanes(width, per):
    level = lax.broadcasted_iota(jnp.int32, (LEV, width), 0)
    lane = lax.broadcasted_iota(jnp.int32, (LEV, width), 1)
    return jnp.where(level == lane // per, F32(1.0), F32(0.0)).astype(BF)


def side_distance(odd):
    row = lax.broadcasted_iota(jnp.int32, (ROWS, 2 * SIDE), 0)
    lane = lax.broadcasted_iota(jnp.int32, (ROWS, 2 * SIDE), 1)
    left = (lane < SIDE) != odd
    place = jnp.where(left, lane % HALO - HALO, lane % HALO + ROWS)
    return place - row


def own_distance():
    row = lax.broadcasted_iota(jnp.int32, (ROWS, OWN), 0)
    lane = lax.broadcasted_iota(jnp.int32, (ROWS, OWN), 1)
    return lane % ROWS - row


def first_kernel(
    group_hbm, weight_hbm, steps_hbm, steps_row_hbm, vert_hbm, lat_hbm, control_hbm, perturb_hbm,
    precision_hbm, innovation_hbm,
    side_ref, back_own_ref, back_side_ref, partial_ref, p_outer_ref, p_inner_ref,
    lat_ref, control_ref, weighted_ref, scale_ref, precision_ref, innovation_ref,
    table, group_ref, weight_ref, steps_ref, steps_row_ref, vert_ref, perturb_ref, sems,
):
    odd = odd_place()
    quarter = precision_ref.shape[0]
    start = pl.multiple_of(lax.rem(lax.axis_index("mem"), XS) * quarter, quarter)
    moves = [
        (vert_hbm, vert_ref),
        (steps_row_hbm, steps_row_ref),
        (steps_hbm, steps_ref),
        (group_hbm, group_ref),
        (weight_hbm, weight_ref),
        (control_hbm, control_ref),
        (lat_hbm, lat_ref),
        (perturb_hbm, perturb_ref),
        (precision_hbm.at[pl.ds(start, quarter)], precision_ref),
        (innovation_hbm.at[pl.ds(start, quarter)], innovation_ref),
    ]
    copies = [pltpu.make_async_copy(a, b, sems.at[i]) for i, (a, b) in enumerate(moves)]
    for copy in copies:
        copy.start()
    for copy in copies[:5]:
        copy.wait()

    vert = vert_ref[...].astype(BF)
    steps_row = steps_row_ref[...].astype(F32).astype(BF)
    lanes_own = spread_lanes(OWN, ROWS)
    lanes_half = spread_lanes(SIDE, HALO)
    lanes_side = jnp.concatenate([lanes_half, lanes_half], axis=1)

    def expand(matrix, lanes, dims=(((1,), (0,)), ((), ()))):
        return lax.dot_general(matrix, lanes, dims, preferred_element_type=F32)

    def forward(lanes, distance):
        n = expand(steps_row, lanes)
        wide = expand(vert, lanes)
        band = weights(n, distance)
        return (wide[:, None, :] * band[None]).reshape(OWN, OWN).astype(BF)

    side_ref[...] = forward(lanes_side, side_distance(odd))
    own = forward(lanes_own, own_distance())

    first_dim = (((0,), (0,)), ((), ()))
    for lanes, distance, out_ref in (
        (lanes_own, own_distance(), back_own_ref),
        (lanes_side, side_distance(odd), back_side_ref),
    ):
        wide = expand(vert, lanes, first_dim)
        for n in range(1, KMAX + 1):
            table[n - 1] = weights(n, distance)
        for l in range(0, LEV, 2):
            pair = [wide[l + i : l + i + 1] * table[steps_ref[l + i] - 1] for i in range(2)]
            out_ref[pl.ds(l * ROWS, 2 * ROWS), :] = jnp.concatenate(pair, axis=0).astype(BF)

    for copy in copies[5:]:
        copy.wait()
    total = jnp.zeros((OWN, LAT), F32)
    for m in range(MEMBERS):
        pack_into(odd, perturb_ref[m], p_outer_ref, p_inner_ref, m)
        weight = weight_ref[group_ref[m]]
        scale_ref[m] = jnp.full((ROWS, LAT), weight)
        weighted = weight * perturb_ref[m].astype(F32)
        weighted_ref[m] = weighted
        mixed = jnp.dot(own, control_ref[m], preferred_element_type=F32).astype(BF)
        total += weighted * jnp.dot(mixed, lat_ref[...], preferred_element_type=F32)
    partial_ref[...] = total


def forward_kernel(side_ref, lat_ref, outer_ref, inner_ref, weighted_ref, partial_ref, out_ref):
    total = partial_ref[...]
    for m in range(MEMBERS):
        mixed = jnp.dot(side_ref[:, :SIDE], outer_ref[m], preferred_element_type=F32)
        mixed += jnp.dot(side_ref[:, SIDE:], inner_ref[m], preferred_element_type=F32)
        local = jnp.dot(mixed.astype(BF), lat_ref[...], preferred_element_type=F32)
        total += weighted_ref[m] * local
    out_ref[...] = total.astype(BF)


def misfit_kernel(some_ref, other_ref, precision_ref, innovation_ref, out_ref):
    increment = some_ref[...].astype(F32) + other_ref[...].astype(F32)
    departure = increment - innovation_ref[...].astype(F32)
    misfit = (precision_ref[...].astype(F32) * departure).astype(BF)
    for j in range(XS):
        out_ref[j] = misfit


def edge_kernel(misfit_ref, outer_ref, inner_ref):
    pack_into(odd_place(), misfit_ref[...], outer_ref, inner_ref, ...)


def sum_kernel(parts_ref, out_ref):
    out_ref[...] = jnp.sum(parts_ref[...].astype(F32), axis=0).astype(BF)


LAST = (((1,), (1,)), ((), ()))


def back_own_kernel(back_own_ref, lat_ref, misfit_ref, weighted_ref, control_ref, out_ref):
    misfit = misfit_ref[...].astype(F32)
    for m in range(MEMBERS):
        back = (weighted_ref[m] * misfit).astype(BF)
        mixed = jnp.dot(back_own_ref[...], back, preferred_element_type=F32).astype(BF)
        latback = lax.dot_general(mixed, lat_ref[...], LAST, preferred_element_type=F32)
        out_ref[m] = control_ref[m].astype(F32) + latback


def back_side_kernel(
    back_side_ref, lat_ref, outer_ref, inner_ref, p_outer_ref, p_inner_ref, scale_ref, base_ref,
    out_hbm, out, sems,
):
    def back(m, p_ref, misfit_ref):
        p = p_ref[m].astype(F32).reshape(SIDE // ROWS, ROWS, LAT)
        weighted = (scale_ref[m][None] * p).reshape(SIDE, LAT)
        return (weighted * misfit_ref[...].astype(F32)).astype(BF)

    half = OWN // 2
    copies = []
    for m in range(MEMBERS):
        from_outer = back(m, p_outer_ref, outer_ref)
        from_inner = back(m, p_inner_ref, inner_ref)
        for h in range(2):
            rows = pl.ds(h * half, half)
            mixed = jnp.dot(back_side_ref[rows, :SIDE], from_outer, preferred_element_type=F32)
            mixed += jnp.dot(back_side_ref[rows, SIDE:], from_inner, preferred_element_type=F32)
            latback = lax.dot_general(
                mixed.astype(BF), lat_ref[...], LAST, preferred_element_type=F32
            )
            out[m, rows, :] = (base_ref[m, rows, :] + latback).astype(BF)
            copy = pltpu.make_async_copy(
                out.at[m, rows], out_hbm.at[m, rows], sems.at[2 * m + h]
            )
            copy.start()
            copies.append(copy)
    for copy in copies:
        copy.wait()


def shards(
    control,
    perturb,
    member_group,
    group_weight,
    step_counts,
    lat_inverse,
    vert_inverse,
    innovation,
    precision,
):
    lons = lax.axis_size("lon")
    within = [(i, i + 1 - 2 * (i % 2)) for i in range(lons)]
    beyond = [(i, (i - 1 + 2 * (i % 2)) % lons) for i in range(lons)]
    mems = lax.axis_size("mem")
    along_x = [list(range(i, i + XS)) for i in range(0, mems, XS)]
    across_y = [(i, (i + XS) % mems) for i in range(mems)]

    def halo(outer, inner):
        from_inner = lax.ppermute(inner, "lon", within)
        return lax.ppermute(outer, "lon", beyond), from_inner

    control = control.reshape(MEMBERS, OWN, LAT)
    perturb = perturb.reshape(MEMBERS, OWN, LAT)
    square = OWN * LAT
    matmul = 2 * OWN * LAT * LAT
    quarter = OWN // XS

    c_outer, c_inner = halo(
        *call(
            pack_kernel, (half_like(MEMBERS),) * 2, (control,), [HBM], 0, 8 * square,
            (pltpu.VMEM((MEMBERS, OWN, LAT), BF), pltpu.SemaphoreType.DMA((MEMBERS * PACK_PARTS,))),
        )
    )
    (
        side, back_own, back_side, partial, p_outer, p_inner, lat, control, weighted, scale, prec,
        innov,
    ) = call(
        first_kernel,
        (
            jax.ShapeDtypeStruct((OWN, 2 * SIDE), BF),
            jax.ShapeDtypeStruct((OWN, OWN), BF),
            jax.ShapeDtypeStruct((OWN, 2 * SIDE), BF),
            jax.ShapeDtypeStruct((OWN, LAT), F32),
            half_like(MEMBERS),
            half_like(MEMBERS),
            jax.ShapeDtypeStruct(lat_inverse.shape, BF),
            jax.ShapeDtypeStruct(control.shape, BF),
            jax.ShapeDtypeStruct(perturb.shape, F32),
            jax.ShapeDtypeStruct((MEMBERS, ROWS, LAT), F32),
            jax.ShapeDtypeStruct((quarter, LAT), BF),
            jax.ShapeDtypeStruct((quarter, LAT), BF),
        ),
        (member_group, group_weight, step_counts, step_counts.reshape(1, LEV), vert_inverse,
         lat_inverse, control, perturb, precision.reshape(OWN, LAT), innovation.reshape(OWN, LAT)),
        [HBM] * 10,
        4 * matmul, 20 * square,
        (
            pltpu.VMEM((KMAX, ROWS, OWN), F32),
            pltpu.SMEM(member_group.shape, jnp.int32),
            pltpu.SMEM(group_weight.shape, F32),
            pltpu.SMEM(step_counts.shape, jnp.int32),
            pltpu.VMEM((1, LEV), jnp.int32),
            pltpu.VMEM(vert_inverse.shape, F32),
            pltpu.VMEM(perturb.shape, BF),
            pltpu.SemaphoreType.DMA((10,)),
        ),
    )
    p_outer, p_inner = halo(p_outer, p_inner)
    partial = call(
        forward_kernel,
        jax.ShapeDtypeStruct((OWN, LAT), BF),
        (side, lat, c_outer, c_inner, weighted, partial),
        [VMEM] * 6,
        4 * matmul, 18 * square,
    )

    parts = lax.all_to_all(
        partial.reshape(XS, quarter, LAT), "mem", 0, 0, axis_index_groups=along_x
    )
    some = call(
        sum_kernel, jax.ShapeDtypeStruct((quarter, LAT), BF), (parts,), [VMEM], 0, 2 * square
    )
    some, p_outer, p_inner = lax.optimization_barrier((some, p_outer, p_inner))
    other = lax.ppermute(some, "mem", across_y)
    misfit = call(
        misfit_kernel,
        jax.ShapeDtypeStruct((XS, quarter, LAT), BF),
        (some, other, prec, innov),
        [VMEM] * 4,
        0, 2 * square,
    )
    misfit = lax.all_to_all(misfit, "mem", 0, 0, axis_index_groups=along_x).reshape(OWN, LAT)

    edge = jax.ShapeDtypeStruct((SIDE, LAT), BF)
    m_outer, m_inner = halo(*call(edge_kernel, (edge, edge), (misfit,), [VMEM], 0, 4 * square))
    base = call(
        back_own_kernel,
        jax.ShapeDtypeStruct((MEMBERS, OWN, LAT), F32),
        (back_own, lat, misfit, weighted, control),
        [VMEM] * 5,
        4 * matmul, 18 * square,
    )
    out = pl.pallas_call(
        back_side_kernel,
        out_shape=jax.ShapeDtypeStruct((MEMBERS, OWN, LAT), BF),
        in_specs=[VMEM] * 8,
        out_specs=HBM,
        scratch_shapes=(
            pltpu.VMEM((MEMBERS, OWN, LAT), BF),
            pltpu.SemaphoreType.DMA((2 * MEMBERS,)),
        ),
        compiler_params=pltpu.CompilerParams(vmem_limit_bytes=VMEM_LIMIT),
        cost_estimate=pl.CostEstimate(
            flops=4 * matmul, bytes_accessed=20 * square, transcendentals=0
        ),
    )(back_side, lat, m_outer, m_inner, p_outer, p_inner, scale, base)
    return out.reshape(MEMBERS, LEV, ROWS, LAT)


def solution(mesh):
    return jax.shard_map(
        shards,
        mesh=mesh,
        in_specs=(
            P("mem", None, "lon", None),
            P("mem", None, "lon", None),
            P("mem"),
            P(),
            P(),
            P(),
            P(),
            P(None, "lon", None),
            P(None, "lon", None),
        ),
        out_specs=P("mem", None, "lon", None),
        check_vma=False,
    )
```

```python
import jax
import jax.numpy as jnp
from jax import lax
from jax.experimental import pallas as pl
from jax.experimental.pallas import tpu as pltpu
from jax.sharding import PartitionSpec as P

LEV = 64
ROWS = 8
LAT = 512
KMAX = 4
HALO = 4
MEMBERS = 2
XS = 4
YS = 4
PACK_PARTS = 4
OWN = LEV * ROWS
SIDE = LEV * HALO

VMEM_LIMIT = 16 * 2**20

BF = jnp.bfloat16
F32 = jnp.float32
VMEM = pl.BlockSpec(memory_space=pltpu.VMEM)
HBM = pl.BlockSpec(memory_space=pltpu.HBM)

BAND = {
    1: {1: 0.5},
    2: {0: 0.5, 2: 0.25},
    3: {1: 0.375, 3: 0.125},
    4: {0: 0.375, 2: 0.25, 4: 0.0625},
}


def in_hbm(x):
    return pltpu.with_memory_space_constraint(x, pltpu.HBM)


def call(kernel, out, operands, specs, flops, moved, scratch=()):
    return pl.pallas_call(
        kernel,
        out_shape=out,
        in_specs=specs,
        out_specs=jax.tree.map(lambda _: VMEM, out),
        scratch_shapes=scratch,
        compiler_params=pltpu.CompilerParams(vmem_limit_bytes=VMEM_LIMIT),
        cost_estimate=pl.CostEstimate(flops=flops, bytes_accessed=moved, transcendentals=0),
    )(*(in_hbm(x) if spec is HBM else x for x, spec in zip(operands, specs)))


def halves(x):
    rows, columns = x.shape
    x = x.reshape(rows // (2 * ROWS), 2, ROWS, columns)
    even, odd = x[:, 0], x[:, 1]
    low = lax.broadcasted_iota(jnp.int32, even.shape, 1) < HALO
    top = jnp.where(low, even, pltpu.roll(odd, HALO, 1))
    bottom = jnp.where(low, pltpu.roll(even, HALO, 1), odd)
    return top.reshape(rows // 2, columns), bottom.reshape(rows // 2, columns)


def odd_place():
    return lax.rem(lax.axis_index("lon"), 2) == 1


def pack_into(odd, x, outer_ref, inner_ref, at):
    top, bottom = halves(x.astype(F32))
    outer_ref[at] = jnp.where(odd, bottom, top).astype(BF)
    inner_ref[at] = jnp.where(odd, top, bottom).astype(BF)


def pack_kernel(x_ref, outer_ref, inner_ref, x, sems):
    odd = odd_place()
    part = OWN // PACK_PARTS
    copies = []
    for i in range(MEMBERS * PACK_PARTS):
        rows = (i // PACK_PARTS, pl.ds(i % PACK_PARTS * part, part))
        copies.append(pltpu.make_async_copy(x_ref.at[rows], x.at[rows], sems.at[i]))
        copies[-1].start()
    for i, copy in enumerate(copies):
        copy.wait()
        m, p = i // PACK_PARTS, i % PACK_PARTS
        pack_into(odd, x[m, pl.ds(p * part, part)], outer_ref, inner_ref, (m, pl.ds(p * part // 2, part // 2)))


def half_like(members):
    return jax.ShapeDtypeStruct((members, SIDE, LAT), BF)


def weights(n, distance):
    total = jnp.zeros(distance.shape, F32)
    for sweeps, band in BAND.items():
        row = jnp.zeros(distance.shape, F32)
        for d, c in band.items():
            row = jnp.where(jnp.abs(distance) == d, jnp.float32(c), row)
        total = jnp.where(n == sweeps, row, total)
    return total


def spread_lanes(width, per):
    level = lax.broadcasted_iota(jnp.int32, (LEV, width), 0)
    lane = lax.broadcasted_iota(jnp.int32, (LEV, width), 1)
    return jnp.where(level == lane // per, F32(1.0), F32(0.0)).astype(BF)


def side_distance(odd):
    row = lax.broadcasted_iota(jnp.int32, (ROWS, 2 * SIDE), 0)
    lane = lax.broadcasted_iota(jnp.int32, (ROWS, 2 * SIDE), 1)
    left = (lane < SIDE) != odd
    place = jnp.where(left, lane % HALO - HALO, lane % HALO + ROWS)
    return place - row


def own_distance():
    row = lax.broadcasted_iota(jnp.int32, (ROWS, OWN), 0)
    lane = lax.broadcasted_iota(jnp.int32, (ROWS, OWN), 1)
    return lane % ROWS - row


def first_kernel(
    group_hbm, weight_hbm, steps_hbm, steps_row_hbm, vert_hbm, lat_hbm, control_hbm, perturb_hbm,
    precision_hbm, innovation_hbm,
    side_ref, back_own_ref, back_side_ref, partial_ref, p_outer_ref, p_inner_ref,
    lat_ref, control_ref, weighted_ref, scale_ref, precision_ref, innovation_ref,
    table, group_ref, weight_ref, steps_ref, steps_row_ref, vert_ref, perturb_ref, sems,
):
    odd = odd_place()
    quarter = precision_ref.shape[0]
    start = pl.multiple_of(lax.rem(lax.axis_index("mem"), XS) * quarter, quarter)
    moves = [
        (vert_hbm, vert_ref),
        (steps_row_hbm, steps_row_ref),
        (steps_hbm, steps_ref),
        (group_hbm, group_ref),
        (weight_hbm, weight_ref),
        (control_hbm, control_ref),
        (lat_hbm, lat_ref),
        (perturb_hbm, perturb_ref),
        (precision_hbm.at[pl.ds(start, quarter)], precision_ref),
        (innovation_hbm.at[pl.ds(start, quarter)], innovation_ref),
    ]
    copies = [pltpu.make_async_copy(a, b, sems.at[i]) for i, (a, b) in enumerate(moves)]
    for copy in copies:
        copy.start()
    for copy in copies[:5]:
        copy.wait()

    vert = vert_ref[...].astype(BF)
    steps_row = steps_row_ref[...].astype(F32).astype(BF)
    lanes_own = spread_lanes(OWN, ROWS)
    lanes_half = spread_lanes(SIDE, HALO)
    lanes_side = jnp.concatenate([lanes_half, lanes_half], axis=1)

    def expand(matrix, lanes, dims=(((1,), (0,)), ((), ()))):
        return lax.dot_general(matrix, lanes, dims, preferred_element_type=F32)

    def forward(lanes, distance):
        n = expand(steps_row, lanes)
        wide = expand(vert, lanes)
        band = weights(n, distance)
        return (wide[:, None, :] * band[None]).reshape(OWN, OWN).astype(BF)

    side_ref[...] = forward(lanes_side, side_distance(odd))
    own = forward(lanes_own, own_distance())

    first_dim = (((0,), (0,)), ((), ()))
    for lanes, distance, out_ref in (
        (lanes_own, own_distance(), back_own_ref),
        (lanes_side, side_distance(odd), back_side_ref),
    ):
        wide = expand(vert, lanes, first_dim)
        for n in range(1, KMAX + 1):
            table[n - 1] = weights(n, distance)
        for l in range(0, LEV, 2):
            pair = [wide[l + i : l + i + 1] * table[steps_ref[l + i] - 1] for i in range(2)]
            out_ref[pl.ds(l * ROWS, 2 * ROWS), :] = jnp.concatenate(pair, axis=0).astype(BF)

    for copy in copies[5:]:
        copy.wait()
    total = jnp.zeros((OWN, LAT), F32)
    for m in range(MEMBERS):
        pack_into(odd, perturb_ref[m], p_outer_ref, p_inner_ref, m)
        weight = weight_ref[group_ref[m]]
        scale_ref[m] = jnp.full((ROWS, LAT), weight)
        weighted = weight * perturb_ref[m].astype(F32)
        weighted_ref[m] = weighted
        mixed = jnp.dot(own, control_ref[m], preferred_element_type=F32).astype(BF)
        total += weighted * jnp.dot(mixed, lat_ref[...], preferred_element_type=F32)
    partial_ref[...] = total


def forward_kernel(side_ref, lat_ref, outer_ref, inner_ref, weighted_ref, partial_ref, out_ref):
    total = partial_ref[...]
    for m in range(MEMBERS):
        mixed = jnp.dot(side_ref[:, :SIDE], outer_ref[m], preferred_element_type=F32)
        mixed += jnp.dot(side_ref[:, SIDE:], inner_ref[m], preferred_element_type=F32)
        local = jnp.dot(mixed.astype(BF), lat_ref[...], preferred_element_type=F32)
        total += weighted_ref[m] * local
    out_ref[...] = total.astype(BF)


def misfit_kernel(some_ref, other_ref, precision_ref, innovation_ref, out_ref):
    increment = some_ref[...].astype(F32) + other_ref[...].astype(F32)
    departure = increment - innovation_ref[...].astype(F32)
    misfit = (precision_ref[...].astype(F32) * departure).astype(BF)
    for j in range(XS):
        out_ref[j] = misfit


def edge_kernel(misfit_ref, outer_ref, inner_ref):
    pack_into(odd_place(), misfit_ref[...], outer_ref, inner_ref, ...)


def sum_kernel(parts_ref, out_ref):
    out_ref[...] = jnp.sum(parts_ref[...].astype(F32), axis=0).astype(BF)


LAST = (((1,), (1,)), ((), ()))


def back_own_kernel(back_own_ref, lat_ref, misfit_ref, weighted_ref, control_ref, out_ref):
    misfit = misfit_ref[...].astype(F32)
    for m in range(MEMBERS):
        back = (weighted_ref[m] * misfit).astype(BF)
        mixed = jnp.dot(back_own_ref[...], back, preferred_element_type=F32).astype(BF)
        latback = lax.dot_general(mixed, lat_ref[...], LAST, preferred_element_type=F32)
        out_ref[m] = control_ref[m].astype(F32) + latback


def back_side_kernel(
    back_side_ref, lat_ref, outer_ref, inner_ref, p_outer_ref, p_inner_ref, scale_ref, base_ref,
    out_hbm, out, sems,
):
    def back(m, p_ref, misfit_ref):
        p = p_ref[m].astype(F32).reshape(SIDE // ROWS, ROWS, LAT)
        weighted = (scale_ref[m][None] * p).reshape(SIDE, LAT)
        return (weighted * misfit_ref[...].astype(F32)).astype(BF)

    half = OWN // 2
    copies = []
    for m in range(MEMBERS):
        from_outer = back(m, p_outer_ref, outer_ref)
        from_inner = back(m, p_inner_ref, inner_ref)
        for h in range(2):
            rows = pl.ds(h * half, half)
            mixed = jnp.dot(back_side_ref[rows, :SIDE], from_outer, preferred_element_type=F32)
            mixed += jnp.dot(back_side_ref[rows, SIDE:], from_inner, preferred_element_type=F32)
            latback = lax.dot_general(
                mixed.astype(BF), lat_ref[...], LAST, preferred_element_type=F32
            )
            out[m, rows, :] = (base_ref[m, rows, :] + latback).astype(BF)
            copy = pltpu.make_async_copy(
                out.at[m, rows], out_hbm.at[m, rows], sems.at[2 * m + h]
            )
            copy.start()
            copies.append(copy)
    for copy in copies:
        copy.wait()


def shards(
    control,
    perturb,
    member_group,
    group_weight,
    step_counts,
    lat_inverse,
    vert_inverse,
    innovation,
    precision,
):
    lons = lax.axis_size("lon")
    within = [(i, i + 1 - 2 * (i % 2)) for i in range(lons)]
    beyond = [(i, (i - 1 + 2 * (i % 2)) % lons) for i in range(lons)]
    mems = lax.axis_size("mem")
    along_x = [list(range(i, i + XS)) for i in range(0, mems, XS)]
    across_y = [(i, (i + XS) % mems) for i in range(mems)]

    run = 2 * YS
    across = [
        (m * lons + i, (m if i // run == j // run else (m + XS) % mems) * lons + j)
        for m in range(mems)
        for i, j in beyond
    ]

    def halo(outer, inner):
        from_inner = lax.ppermute(inner, "lon", within)
        return lax.ppermute(outer, "lon", beyond), from_inner

    def misfit_halo(outer, inner):
        from_inner = lax.ppermute(inner, "lon", within)
        return lax.ppermute(outer, ("mem", "lon"), across), from_inner

    control = control.reshape(MEMBERS, OWN, LAT)
    perturb = perturb.reshape(MEMBERS, OWN, LAT)
    square = OWN * LAT
    matmul = 2 * OWN * LAT * LAT
    quarter = OWN // XS

    c_outer, c_inner = halo(
        *call(
            pack_kernel, (half_like(MEMBERS),) * 2, (control,), [HBM], 0, 8 * square,
            (pltpu.VMEM((MEMBERS, OWN, LAT), BF), pltpu.SemaphoreType.DMA((MEMBERS * PACK_PARTS,))),
        )
    )
    (
        side, back_own, back_side, partial, p_outer, p_inner, lat, control, weighted, scale, prec,
        innov,
    ) = call(
        first_kernel,
        (
            jax.ShapeDtypeStruct((OWN, 2 * SIDE), BF),
            jax.ShapeDtypeStruct((OWN, OWN), BF),
            jax.ShapeDtypeStruct((OWN, 2 * SIDE), BF),
            jax.ShapeDtypeStruct((OWN, LAT), F32),
            half_like(MEMBERS),
            half_like(MEMBERS),
            jax.ShapeDtypeStruct(lat_inverse.shape, BF),
            jax.ShapeDtypeStruct(control.shape, BF),
            jax.ShapeDtypeStruct(perturb.shape, F32),
            jax.ShapeDtypeStruct((MEMBERS, ROWS, LAT), F32),
            jax.ShapeDtypeStruct((quarter, LAT), BF),
            jax.ShapeDtypeStruct((quarter, LAT), BF),
        ),
        (member_group, group_weight, step_counts, step_counts.reshape(1, LEV), vert_inverse,
         lat_inverse, control, perturb, precision.reshape(OWN, LAT), innovation.reshape(OWN, LAT)),
        [HBM] * 10,
        4 * matmul, 20 * square,
        (
            pltpu.VMEM((KMAX, ROWS, OWN), F32),
            pltpu.SMEM(member_group.shape, jnp.int32),
            pltpu.SMEM(group_weight.shape, F32),
            pltpu.SMEM(step_counts.shape, jnp.int32),
            pltpu.VMEM((1, LEV), jnp.int32),
            pltpu.VMEM(vert_inverse.shape, F32),
            pltpu.VMEM(perturb.shape, BF),
            pltpu.SemaphoreType.DMA((10,)),
        ),
    )
    p_outer, p_inner = halo(p_outer, p_inner)
    partial = call(
        forward_kernel,
        jax.ShapeDtypeStruct((OWN, LAT), BF),
        (side, lat, c_outer, c_inner, weighted, partial),
        [VMEM] * 6,
        4 * matmul, 18 * square,
    )

    parts = lax.all_to_all(
        partial.reshape(XS, quarter, LAT), "mem", 0, 0, axis_index_groups=along_x
    )
    some = call(
        sum_kernel, jax.ShapeDtypeStruct((quarter, LAT), BF), (parts,), [VMEM], 0, 2 * square
    )
    some, p_outer, p_inner = lax.optimization_barrier((some, p_outer, p_inner))
    other = lax.ppermute(some, "mem", across_y)
    misfit = call(
        misfit_kernel,
        jax.ShapeDtypeStruct((XS, quarter, LAT), BF),
        (some, other, prec, innov),
        [VMEM] * 4,
        0, 2 * square,
    )
    misfit = lax.all_to_all(misfit, "mem", 0, 0, axis_index_groups=along_x).reshape(OWN, LAT)

    edge = jax.ShapeDtypeStruct((SIDE, LAT), BF)
    m_outer, m_inner = misfit_halo(
        *call(edge_kernel, (edge, edge), (misfit,), [VMEM], 0, 4 * square)
    )
    base = call(
        back_own_kernel,
        jax.ShapeDtypeStruct((MEMBERS, OWN, LAT), F32),
        (back_own, lat, misfit, weighted, control),
        [VMEM] * 5,
        4 * matmul, 18 * square,
    )
    out = pl.pallas_call(
        back_side_kernel,
        out_shape=jax.ShapeDtypeStruct((MEMBERS, OWN, LAT), BF),
        in_specs=[VMEM] * 8,
        out_specs=HBM,
        scratch_shapes=(
            pltpu.VMEM((MEMBERS, OWN, LAT), BF),
            pltpu.SemaphoreType.DMA((2 * MEMBERS,)),
        ),
        compiler_params=pltpu.CompilerParams(vmem_limit_bytes=VMEM_LIMIT),
        cost_estimate=pl.CostEstimate(
            flops=4 * matmul, bytes_accessed=20 * square, transcendentals=0
        ),
    )(back_side, lat, m_outer, m_inner, p_outer, p_inner, scale, base)
    return out.reshape(MEMBERS, LEV, ROWS, LAT)


def solution(mesh):
    return jax.shard_map(
        shards,
        mesh=mesh,
        in_specs=(
            P("mem", None, "lon", None),
            P("mem", None, "lon", None),
            P("mem"),
            P(),
            P(),
            P(),
            P(),
            P(None, "lon", None),
            P(None, "lon", None),
        ),
        out_specs=P("mem", None, "lon", None),
        check_vma=False,
    )
```

```python
import functools

import jax
import jax.numpy as jnp
from jax import lax
from jax.experimental import pallas as pl
from jax.experimental.pallas import tpu as pltpu
from jax.sharding import PartitionSpec as P

LEV = 64
ROWS = 8
LAT = 512
KMAX = 4
HALO = 4
MEMBERS = 2
XS = 4
YS = 4
PACK_PARTS = 2
OWN = LEV * ROWS
SIDE = LEV * HALO

VMEM_LIMIT = 16 * 2**20

BF = jnp.bfloat16
F32 = jnp.float32
VMEM = pl.BlockSpec(memory_space=pltpu.VMEM)
HBM = pl.BlockSpec(memory_space=pltpu.HBM)

BAND = {
    1: {1: 0.5},
    2: {0: 0.5, 2: 0.25},
    3: {1: 0.375, 3: 0.125},
    4: {0: 0.375, 2: 0.25, 4: 0.0625},
}


def in_hbm(x):
    return pltpu.with_memory_space_constraint(x, pltpu.HBM)


def call(kernel, out, operands, specs, flops, moved, scratch=()):
    return pl.pallas_call(
        kernel,
        out_shape=out,
        in_specs=specs,
        out_specs=jax.tree.map(lambda _: VMEM, out),
        scratch_shapes=scratch,
        compiler_params=pltpu.CompilerParams(vmem_limit_bytes=VMEM_LIMIT),
        cost_estimate=pl.CostEstimate(flops=flops, bytes_accessed=moved, transcendentals=0),
    )(*(in_hbm(x) if spec is HBM else x for x, spec in zip(operands, specs)))


def halves(x):
    rows, columns = x.shape
    x = x.reshape(rows // (2 * ROWS), 2, ROWS, columns)
    even, odd = x[:, 0], x[:, 1]
    low = lax.broadcasted_iota(jnp.int32, even.shape, 1) < HALO
    top = jnp.where(low, even, pltpu.roll(odd, HALO, 1))
    bottom = jnp.where(low, pltpu.roll(even, HALO, 1), odd)
    return top.reshape(rows // 2, columns), bottom.reshape(rows // 2, columns)


def waits(lons):
    lon = lax.axis_index("lon")
    return (lon > lons - 2 * YS) & (lon < lons - 1)


def odd_place():
    return lax.rem(lax.axis_index("lon"), 2) == 1


def pack_into(odd, x, outer_ref, inner_ref, at):
    top, bottom = halves(x.astype(F32))
    outer_ref[at] = jnp.where(odd, bottom, top).astype(BF)
    inner_ref[at] = jnp.where(odd, top, bottom).astype(BF)


def pack_kernel(x_ref, outer_ref, inner_ref, again_ref, x, sems):
    odd = odd_place()
    part = OWN // PACK_PARTS
    copies = []
    for i in range(MEMBERS * PACK_PARTS):
        rows = (i // PACK_PARTS, pl.ds(i % PACK_PARTS * part, part))
        copies.append(pltpu.make_async_copy(x_ref.at[rows], x.at[rows], sems.at[i]))
        copies[-1].start()
    for i, copy in enumerate(copies):
        copy.wait()
        m, p = i // PACK_PARTS, i % PACK_PARTS
        at = (m, pl.ds(p * part // 2, part // 2))
        pack_into(odd, x[m, pl.ds(p * part, part)], outer_ref, inner_ref, at)
        again_ref[at] = outer_ref[at]


def half_like(members):
    return jax.ShapeDtypeStruct((members, SIDE, LAT), BF)


def weights(n, distance):
    total = jnp.zeros(distance.shape, F32)
    for sweeps, band in BAND.items():
        row = jnp.zeros(distance.shape, F32)
        for d, c in band.items():
            row = jnp.where(jnp.abs(distance) == d, jnp.float32(c), row)
        total = jnp.where(n == sweeps, row, total)
    return total


def spread_lanes(width, per):
    level = lax.broadcasted_iota(jnp.int32, (LEV, width), 0)
    lane = lax.broadcasted_iota(jnp.int32, (LEV, width), 1)
    return jnp.where(level == lane // per, F32(1.0), F32(0.0)).astype(BF)


def side_distance(odd):
    row = lax.broadcasted_iota(jnp.int32, (ROWS, 2 * SIDE), 0)
    lane = lax.broadcasted_iota(jnp.int32, (ROWS, 2 * SIDE), 1)
    left = (lane < SIDE) != odd
    place = jnp.where(left, lane % HALO - HALO, lane % HALO + ROWS)
    return place - row


def own_distance():
    row = lax.broadcasted_iota(jnp.int32, (ROWS, OWN), 0)
    lane = lax.broadcasted_iota(jnp.int32, (ROWS, OWN), 1)
    return lane % ROWS - row


def first_kernel(
    group_hbm, weight_hbm, steps_hbm, steps_row_hbm, vert_hbm, lat_hbm, control_hbm, perturb_hbm,
    precision_hbm, innovation_hbm,
    side_ref, back_own_ref, back_side_ref, partial_ref, p_outer_ref, p_inner_ref,
    lat_ref, control_ref, weighted_ref, scale_ref, precision_ref, innovation_ref,
    table, group_ref, weight_ref, steps_ref, steps_row_ref, vert_ref, perturb_ref, sems,
):
    odd = odd_place()
    quarter = precision_ref.shape[0]
    start = pl.multiple_of(lax.rem(lax.axis_index("mem"), XS) * quarter, quarter)
    moves = [
        (vert_hbm, vert_ref),
        (steps_row_hbm, steps_row_ref),
        (steps_hbm, steps_ref),
        (group_hbm, group_ref),
        (weight_hbm, weight_ref),
        (control_hbm, control_ref),
        (lat_hbm, lat_ref),
        (perturb_hbm, perturb_ref),
        (precision_hbm.at[pl.ds(start, quarter)], precision_ref),
        (innovation_hbm.at[pl.ds(start, quarter)], innovation_ref),
    ]
    copies = [pltpu.make_async_copy(a, b, sems.at[i]) for i, (a, b) in enumerate(moves)]
    for copy in copies:
        copy.start()
    for copy in copies[:5]:
        copy.wait()

    vert = vert_ref[...].astype(BF)
    steps_row = steps_row_ref[...].astype(F32).astype(BF)
    lanes_own = spread_lanes(OWN, ROWS)
    lanes_half = spread_lanes(SIDE, HALO)
    lanes_side = jnp.concatenate([lanes_half, lanes_half], axis=1)

    def expand(matrix, lanes, dims=(((1,), (0,)), ((), ()))):
        return lax.dot_general(matrix, lanes, dims, preferred_element_type=F32)

    def forward(lanes, distance):
        n = expand(steps_row, lanes)
        wide = expand(vert, lanes)
        band = weights(n, distance)
        return (wide[:, None, :] * band[None]).reshape(OWN, OWN).astype(BF)

    side_ref[...] = forward(lanes_side, side_distance(odd))
    own = forward(lanes_own, own_distance())

    first_dim = (((0,), (0,)), ((), ()))
    for lanes, distance, out_ref in (
        (lanes_own, own_distance(), back_own_ref),
        (lanes_side, side_distance(odd), back_side_ref),
    ):
        wide = expand(vert, lanes, first_dim)
        for n in range(1, KMAX + 1):
            table[n - 1] = weights(n, distance)
        for l in range(0, LEV, 2):
            pair = [wide[l + i : l + i + 1] * table[steps_ref[l + i] - 1] for i in range(2)]
            out_ref[pl.ds(l * ROWS, 2 * ROWS), :] = jnp.concatenate(pair, axis=0).astype(BF)

    for copy in copies[5:]:
        copy.wait()
    total = jnp.zeros((OWN, LAT), F32)
    for m in range(MEMBERS):
        pack_into(odd, perturb_ref[m], p_outer_ref, p_inner_ref, m)
        weight = weight_ref[group_ref[m]]
        scale_ref[m] = jnp.full((ROWS, LAT), weight)
        weighted = weight * perturb_ref[m].astype(F32)
        weighted_ref[m] = weighted
        mixed = jnp.dot(own, control_ref[m], preferred_element_type=F32).astype(BF)
        total += weighted * jnp.dot(mixed, lat_ref[...], preferred_element_type=F32)
    partial_ref[...] = total


def forward_kernel(
    lons, side_ref, lat_ref, outer_ref, inner_ref, later_ref, weighted_ref, partial_ref, out_ref
):
    late = waits(lons)
    total = partial_ref[...]
    for m in range(MEMBERS):
        outer = jnp.where(late, later_ref[m], outer_ref[m])
        mixed = jnp.dot(side_ref[:, :SIDE], outer, preferred_element_type=F32)
        mixed += jnp.dot(side_ref[:, SIDE:], inner_ref[m], preferred_element_type=F32)
        local = jnp.dot(mixed.astype(BF), lat_ref[...], preferred_element_type=F32)
        total += weighted_ref[m] * local
    out_ref[...] = total.astype(BF)


def misfit_kernel(some_ref, other_ref, precision_ref, innovation_ref, out_ref):
    increment = some_ref[...].astype(F32) + other_ref[...].astype(F32)
    departure = increment - innovation_ref[...].astype(F32)
    misfit = (precision_ref[...].astype(F32) * departure).astype(BF)
    for j in range(XS):
        out_ref[j] = misfit


def edge_kernel(misfit_ref, outer_ref, inner_ref):
    pack_into(odd_place(), misfit_ref[...], outer_ref, inner_ref, ...)


def sum_kernel(parts_ref, out_ref):
    out_ref[...] = jnp.sum(parts_ref[...].astype(F32), axis=0).astype(BF)


LAST = (((1,), (1,)), ((), ()))


def back_own_kernel(back_own_ref, lat_ref, misfit_ref, weighted_ref, control_ref, out_ref):
    misfit = misfit_ref[...].astype(F32)
    for m in range(MEMBERS):
        back = (weighted_ref[m] * misfit).astype(BF)
        mixed = jnp.dot(back_own_ref[...], back, preferred_element_type=F32).astype(BF)
        latback = lax.dot_general(mixed, lat_ref[...], LAST, preferred_element_type=F32)
        out_ref[m] = control_ref[m].astype(F32) + latback


def back_side_kernel(
    back_side_ref, lat_ref, outer_ref, inner_ref, p_outer_ref, p_inner_ref, scale_ref, base_ref,
    out_hbm, out, sems,
):
    def back(m, p_ref, misfit_ref):
        p = p_ref[m].astype(F32).reshape(SIDE // ROWS, ROWS, LAT)
        weighted = (scale_ref[m][None] * p).reshape(SIDE, LAT)
        return (weighted * misfit_ref[...].astype(F32)).astype(BF)

    half = OWN // 2
    copies = []
    for m in range(MEMBERS):
        from_outer = back(m, p_outer_ref, outer_ref)
        from_inner = back(m, p_inner_ref, inner_ref)
        for h in range(2):
            rows = pl.ds(h * half, half)
            mixed = jnp.dot(back_side_ref[rows, :SIDE], from_outer, preferred_element_type=F32)
            mixed += jnp.dot(back_side_ref[rows, SIDE:], from_inner, preferred_element_type=F32)
            latback = lax.dot_general(
                mixed.astype(BF), lat_ref[...], LAST, preferred_element_type=F32
            )
            out[m, rows, :] = (base_ref[m, rows, :] + latback).astype(BF)
            copy = pltpu.make_async_copy(
                out.at[m, rows], out_hbm.at[m, rows], sems.at[2 * m + h]
            )
            copy.start()
            copies.append(copy)
    for copy in copies:
        copy.wait()


def shards(
    control,
    perturb,
    member_group,
    group_weight,
    step_counts,
    lat_inverse,
    vert_inverse,
    innovation,
    precision,
):
    lons = lax.axis_size("lon")
    within = [(i, i + 1 - 2 * (i % 2)) for i in range(lons)]
    beyond = [(i, (i - 1 + 2 * (i % 2)) % lons) for i in range(lons)]
    mems = lax.axis_size("mem")
    along_x = [list(range(i, i + XS)) for i in range(0, mems, XS)]
    across_y = [(i, (i + XS) % mems) for i in range(mems)]

    run = 2 * YS
    across = [
        (m * lons + i, (m if i // run == j // run else (m + XS) % mems) * lons + j)
        for m in range(mems)
        for i, j in beyond
    ]

    later = [(i, j) for i, j in beyond if lons - run < i < lons - 1]
    sooner = [(i, i) if (i, j) in later else (i, j) for i, j in beyond]

    def halo(outer, inner, again):
        from_inner = lax.ppermute(inner, "lon", within)
        from_later = lax.ppermute(again, "lon", later)
        return lax.ppermute(outer, "lon", sooner), from_inner, from_later

    def misfit_halo(outer, inner):
        from_inner = lax.ppermute(inner, "lon", within)
        return lax.ppermute(outer, ("mem", "lon"), across), from_inner

    control = control.reshape(MEMBERS, OWN, LAT)
    perturb = perturb.reshape(MEMBERS, OWN, LAT)
    square = OWN * LAT
    matmul = 2 * OWN * LAT * LAT
    quarter = OWN // XS

    c_outer, c_inner, c_later = halo(
        *call(
            pack_kernel, (half_like(MEMBERS),) * 3, (control,), [HBM], 0, 8 * square,
            (pltpu.VMEM((MEMBERS, OWN, LAT), BF), pltpu.SemaphoreType.DMA((MEMBERS * PACK_PARTS,))),
        )
    )
    (
        side, back_own, back_side, partial, p_outer, p_inner, lat, control, weighted, scale, prec,
        innov,
    ) = call(
        first_kernel,
        (
            jax.ShapeDtypeStruct((OWN, 2 * SIDE), BF),
            jax.ShapeDtypeStruct((OWN, OWN), BF),
            jax.ShapeDtypeStruct((OWN, 2 * SIDE), BF),
            jax.ShapeDtypeStruct((OWN, LAT), F32),
            half_like(MEMBERS),
            half_like(MEMBERS),
            jax.ShapeDtypeStruct(lat_inverse.shape, BF),
            jax.ShapeDtypeStruct(control.shape, BF),
            jax.ShapeDtypeStruct(perturb.shape, F32),
            jax.ShapeDtypeStruct((MEMBERS, ROWS, LAT), F32),
            jax.ShapeDtypeStruct((quarter, LAT), BF),
            jax.ShapeDtypeStruct((quarter, LAT), BF),
        ),
        (member_group, group_weight, step_counts, step_counts.reshape(1, LEV), vert_inverse,
         lat_inverse, control, perturb, precision.reshape(OWN, LAT), innovation.reshape(OWN, LAT)),
        [HBM] * 10,
        4 * matmul, 20 * square,
        (
            pltpu.VMEM((KMAX, ROWS, OWN), F32),
            pltpu.SMEM(member_group.shape, jnp.int32),
            pltpu.SMEM(group_weight.shape, F32),
            pltpu.SMEM(step_counts.shape, jnp.int32),
            pltpu.VMEM((1, LEV), jnp.int32),
            pltpu.VMEM(vert_inverse.shape, F32),
            pltpu.VMEM(perturb.shape, BF),
            pltpu.SemaphoreType.DMA((10,)),
        ),
    )
    p_inner = lax.ppermute(p_inner, "lon", within)
    partial = call(
        functools.partial(forward_kernel, lons),
        jax.ShapeDtypeStruct((OWN, LAT), BF),
        (side, lat, c_outer, c_inner, c_later, weighted, partial),
        [VMEM] * 7,
        4 * matmul, 18 * square,
    )

    parts = lax.all_to_all(
        partial.reshape(XS, quarter, LAT), "mem", 0, 0, axis_index_groups=along_x
    )
    some = call(
        sum_kernel, jax.ShapeDtypeStruct((quarter, LAT), BF), (parts,), [VMEM], 0, 2 * square
    )
    some, p_inner, p_outer = lax.optimization_barrier((some, p_inner, p_outer))
    other = lax.ppermute(some, "mem", across_y)
    p_outer = lax.ppermute(p_outer, "lon", beyond)
    misfit = call(
        misfit_kernel,
        jax.ShapeDtypeStruct((XS, quarter, LAT), BF),
        (some, other, prec, innov),
        [VMEM] * 4,
        0, 2 * square,
    )
    misfit = lax.all_to_all(misfit, "mem", 0, 0, axis_index_groups=along_x).reshape(OWN, LAT)

    edge = jax.ShapeDtypeStruct((SIDE, LAT), BF)
    m_outer, m_inner = call(edge_kernel, (edge, edge), (misfit,), [VMEM], 0, 4 * square)
    m_inner, p_outer = lax.optimization_barrier((m_inner, p_outer))
    m_outer, m_inner = misfit_halo(m_outer, m_inner)
    base = call(
        back_own_kernel,
        jax.ShapeDtypeStruct((MEMBERS, OWN, LAT), F32),
        (back_own, lat, misfit, weighted, control),
        [VMEM] * 5,
        4 * matmul, 18 * square,
    )
    out = pl.pallas_call(
        back_side_kernel,
        out_shape=jax.ShapeDtypeStruct((MEMBERS, OWN, LAT), BF),
        in_specs=[VMEM] * 8,
        out_specs=HBM,
        scratch_shapes=(
            pltpu.VMEM((MEMBERS, OWN, LAT), BF),
            pltpu.SemaphoreType.DMA((2 * MEMBERS,)),
        ),
        compiler_params=pltpu.CompilerParams(vmem_limit_bytes=VMEM_LIMIT),
        cost_estimate=pl.CostEstimate(
            flops=4 * matmul, bytes_accessed=20 * square, transcendentals=0
        ),
    )(back_side, lat, m_outer, m_inner, p_outer, p_inner, scale, base)
    return out.reshape(MEMBERS, LEV, ROWS, LAT)


def solution(mesh):
    return jax.shard_map(
        shards,
        mesh=mesh,
        in_specs=(
            P("mem", None, "lon", None),
            P("mem", None, "lon", None),
            P("mem"),
            P(),
            P(),
            P(),
            P(),
            P(None, "lon", None),
            P(None, "lon", None),
        ),
        out_specs=P("mem", None, "lon", None),
        check_vma=False,
    )
```

```python
import functools

import jax
import jax.numpy as jnp
from jax import lax
from jax.experimental import pallas as pl
from jax.experimental.pallas import tpu as pltpu
from jax.sharding import PartitionSpec as P

LEV = 64
ROWS = 8
LAT = 512
KMAX = 4
HALO = 4
MEMBERS = 2
XS = 4
YS = 4
PACK_PARTS = 2
OWN = LEV * ROWS
SIDE = LEV * HALO

VMEM_LIMIT = 16 * 2**20

BF = jnp.bfloat16
F32 = jnp.float32
VMEM = pl.BlockSpec(memory_space=pltpu.VMEM)
HBM = pl.BlockSpec(memory_space=pltpu.HBM)

BAND = {
    1: {1: 0.5},
    2: {0: 0.5, 2: 0.25},
    3: {1: 0.375, 3: 0.125},
    4: {0: 0.375, 2: 0.25, 4: 0.0625},
}


def in_hbm(x):
    return pltpu.with_memory_space_constraint(x, pltpu.HBM)


def call(kernel, out, operands, specs, flops, moved, scratch=()):
    return pl.pallas_call(
        kernel,
        out_shape=out,
        in_specs=specs,
        out_specs=jax.tree.map(lambda _: VMEM, out),
        scratch_shapes=scratch,
        compiler_params=pltpu.CompilerParams(vmem_limit_bytes=VMEM_LIMIT),
        cost_estimate=pl.CostEstimate(flops=flops, bytes_accessed=moved, transcendentals=0),
    )(*(in_hbm(x) if spec is HBM else x for x, spec in zip(operands, specs)))


def halves(x):
    rows, columns = x.shape
    x = x.reshape(rows // (2 * ROWS), 2, ROWS, columns)
    even, odd = x[:, 0], x[:, 1]
    low = lax.broadcasted_iota(jnp.int32, even.shape, 1) < HALO
    top = jnp.where(low, even, pltpu.roll(odd, HALO, 1))
    bottom = jnp.where(low, pltpu.roll(even, HALO, 1), odd)
    return top.reshape(rows // 2, columns), bottom.reshape(rows // 2, columns)


def waits(lons):
    lon = lax.axis_index("lon")
    return (lon > lons - 2 * YS) & (lon < lons - 1)


def odd_place():
    return lax.rem(lax.axis_index("lon"), 2) == 1


def pack_into(odd, x, outer_ref, inner_ref, at):
    top, bottom = halves(x.astype(F32))
    outer_ref[at] = jnp.where(odd, bottom, top).astype(BF)
    inner_ref[at] = jnp.where(odd, top, bottom).astype(BF)


def pack_kernel(x_ref, outer_ref, inner_ref, again_ref, x, sems):
    odd = odd_place()
    part = OWN // PACK_PARTS
    copies = []
    for i in range(MEMBERS * PACK_PARTS):
        rows = (i // PACK_PARTS, pl.ds(i % PACK_PARTS * part, part))
        copies.append(pltpu.make_async_copy(x_ref.at[rows], x.at[rows], sems.at[i]))
        copies[-1].start()
    for i, copy in enumerate(copies):
        copy.wait()
        m, p = i // PACK_PARTS, i % PACK_PARTS
        at = (m, pl.ds(p * part // 2, part // 2))
        pack_into(odd, x[m, pl.ds(p * part, part)], outer_ref, inner_ref, at)
        again_ref[at] = outer_ref[at]


def half_like(members):
    return jax.ShapeDtypeStruct((members, SIDE, LAT), BF)


def weights(n, distance):
    total = jnp.zeros(distance.shape, F32)
    for sweeps, band in BAND.items():
        row = jnp.zeros(distance.shape, F32)
        for d, c in band.items():
            row = jnp.where(jnp.abs(distance) == d, jnp.float32(c), row)
        total = jnp.where(n == sweeps, row, total)
    return total


def spread_lanes(width, per):
    level = lax.broadcasted_iota(jnp.int32, (LEV, width), 0)
    lane = lax.broadcasted_iota(jnp.int32, (LEV, width), 1)
    return jnp.where(level == lane // per, F32(1.0), F32(0.0)).astype(BF)


def side_distance(odd):
    row = lax.broadcasted_iota(jnp.int32, (ROWS, 2 * SIDE), 0)
    lane = lax.broadcasted_iota(jnp.int32, (ROWS, 2 * SIDE), 1)
    left = (lane < SIDE) != odd
    place = jnp.where(left, lane % HALO - HALO, lane % HALO + ROWS)
    return place - row


def own_distance():
    row = lax.broadcasted_iota(jnp.int32, (ROWS, OWN), 0)
    lane = lax.broadcasted_iota(jnp.int32, (ROWS, OWN), 1)
    return lane % ROWS - row


def first_kernel(
    group_hbm, weight_hbm, steps_hbm, steps_row_hbm, vert_hbm, lat_hbm, control_hbm, perturb_hbm,
    precision_hbm, innovation_hbm,
    side_ref, back_own_ref, back_side_ref, partial_ref, p_outer_ref, p_inner_ref,
    lat_ref, control_ref, weighted_ref, scale_ref, precision_ref, innovation_ref,
    table, group_ref, weight_ref, steps_ref, steps_row_ref, vert_ref, perturb_ref, sems,
):
    odd = odd_place()
    quarter = precision_ref.shape[0]
    start = pl.multiple_of(lax.rem(lax.axis_index("mem"), XS) * quarter, quarter)
    moves = [
        (vert_hbm, vert_ref),
        (steps_row_hbm, steps_row_ref),
        (steps_hbm, steps_ref),
        (group_hbm, group_ref),
        (weight_hbm, weight_ref),
        (control_hbm, control_ref),
        (lat_hbm, lat_ref),
        (perturb_hbm, perturb_ref),
        (precision_hbm.at[pl.ds(start, quarter)], precision_ref),
        (innovation_hbm.at[pl.ds(start, quarter)], innovation_ref),
    ]
    copies = [pltpu.make_async_copy(a, b, sems.at[i]) for i, (a, b) in enumerate(moves)]
    for copy in copies:
        copy.start()
    for copy in copies[:5]:
        copy.wait()

    vert = vert_ref[...].astype(BF)
    steps_row = steps_row_ref[...].astype(F32).astype(BF)
    lanes_own = spread_lanes(OWN, ROWS)
    lanes_half = spread_lanes(SIDE, HALO)
    lanes_side = jnp.concatenate([lanes_half, lanes_half], axis=1)

    def expand(matrix, lanes, dims=(((1,), (0,)), ((), ()))):
        return lax.dot_general(matrix, lanes, dims, preferred_element_type=F32)

    def forward(lanes, distance):
        n = expand(steps_row, lanes)
        wide = expand(vert, lanes)
        band = weights(n, distance)
        return (wide[:, None, :] * band[None]).reshape(OWN, OWN).astype(BF)

    side_ref[...] = forward(lanes_side, side_distance(odd))
    own = forward(lanes_own, own_distance())

    first_dim = (((0,), (0,)), ((), ()))
    for lanes, distance, out_ref in (
        (lanes_own, own_distance(), back_own_ref),
        (lanes_side, side_distance(odd), back_side_ref),
    ):
        wide = expand(vert, lanes, first_dim)
        for n in range(1, KMAX + 1):
            table[n - 1] = weights(n, distance)
        for l in range(0, LEV, 2):
            pair = [wide[l + i : l + i + 1] * table[steps_ref[l + i] - 1] for i in range(2)]
            out_ref[pl.ds(l * ROWS, 2 * ROWS), :] = jnp.concatenate(pair, axis=0).astype(BF)

    for copy in copies[5:]:
        copy.wait()
    total = jnp.zeros((OWN, LAT), F32)
    for m in range(MEMBERS):
        pack_into(odd, perturb_ref[m], p_outer_ref, p_inner_ref, m)
        weight = weight_ref[group_ref[m]]
        scale_ref[m] = jnp.full((ROWS, LAT), weight)
        weighted = weight * perturb_ref[m].astype(F32)
        weighted_ref[m] = weighted
        mixed = jnp.dot(own, control_ref[m], preferred_element_type=F32).astype(BF)
        total += weighted * jnp.dot(mixed, lat_ref[...], preferred_element_type=F32)
    partial_ref[...] = total


def forward_kernel(
    lons, side_ref, lat_ref, outer_ref, inner_ref, later_ref, weighted_ref, partial_ref, out_ref
):
    late = waits(lons)
    total = partial_ref[...]
    for m in range(MEMBERS):
        outer = jnp.where(late, later_ref[m], outer_ref[m])
        mixed = jnp.dot(side_ref[:, :SIDE], outer, preferred_element_type=F32)
        mixed += jnp.dot(side_ref[:, SIDE:], inner_ref[m], preferred_element_type=F32)
        local = jnp.dot(mixed.astype(BF), lat_ref[...], preferred_element_type=F32)
        total += weighted_ref[m] * local
    out_ref[...] = total.astype(BF)


def misfit_kernel(some_ref, other_ref, precision_ref, innovation_ref, out_ref):
    increment = some_ref[...].astype(F32) + other_ref[...].astype(F32)
    departure = increment - innovation_ref[...].astype(F32)
    misfit = (precision_ref[...].astype(F32) * departure).astype(BF)
    for j in range(XS):
        out_ref[j] = misfit


def edge_kernel(misfit_ref, outer_ref, inner_ref):
    pack_into(odd_place(), misfit_ref[...], outer_ref, inner_ref, ...)


def sum_kernel(parts_ref, out_ref):
    out_ref[...] = jnp.sum(parts_ref[...].astype(F32), axis=0).astype(BF)


LAST = (((1,), (1,)), ((), ()))


def back_own_kernel(back_own_ref, lat_ref, misfit_ref, weighted_ref, control_ref, out_ref):
    misfit = misfit_ref[...].astype(F32)
    for m in range(MEMBERS):
        back = (weighted_ref[m] * misfit).astype(BF)
        mixed = jnp.dot(back_own_ref[...], back, preferred_element_type=F32).astype(BF)
        latback = lax.dot_general(mixed, lat_ref[...], LAST, preferred_element_type=F32)
        out_ref[m] = control_ref[m].astype(F32) + latback


def back_side_kernel(
    back_side_ref, lat_ref, outer_ref, inner_ref, p_outer_ref, p_inner_ref, scale_ref, base_ref,
    out_hbm, out, sems,
):
    def back(m, p_ref, misfit_ref):
        p = p_ref[m].astype(F32).reshape(SIDE // ROWS, ROWS, LAT)
        weighted = (scale_ref[m][None] * p).reshape(SIDE, LAT)
        return (weighted * misfit_ref[...].astype(F32)).astype(BF)

    half = OWN // 2
    copies = []
    for m in range(MEMBERS):
        from_outer = back(m, p_outer_ref, outer_ref)
        from_inner = back(m, p_inner_ref, inner_ref)
        for h in range(2):
            rows = pl.ds(h * half, half)
            mixed = jnp.dot(back_side_ref[rows, :SIDE], from_outer, preferred_element_type=F32)
            mixed += jnp.dot(back_side_ref[rows, SIDE:], from_inner, preferred_element_type=F32)
            latback = lax.dot_general(
                mixed.astype(BF), lat_ref[...], LAST, preferred_element_type=F32
            )
            out[m, rows, :] = (base_ref[m, rows, :] + latback).astype(BF)
            copy = pltpu.make_async_copy(
                out.at[m, rows], out_hbm.at[m, rows], sems.at[2 * m + h]
            )
            copy.start()
            copies.append(copy)
    for copy in copies:
        copy.wait()


def shards(
    control,
    perturb,
    member_group,
    group_weight,
    step_counts,
    lat_inverse,
    vert_inverse,
    innovation,
    precision,
):
    lons = lax.axis_size("lon")
    within = [(i, i + 1 - 2 * (i % 2)) for i in range(lons)]
    beyond = [(i, (i - 1 + 2 * (i % 2)) % lons) for i in range(lons)]
    mems = lax.axis_size("mem")
    along_x = [list(range(i, i + XS)) for i in range(0, mems, XS)]
    across_y = [(i, (i + XS) % mems) for i in range(mems)]

    run = 2 * YS
    across = [
        (m * lons + i, (m if i // run == j // run else (m + XS) % mems) * lons + j)
        for m in range(mems)
        for i, j in beyond
    ]

    later = [(i, j) for i, j in beyond if lons - run < i < lons - 1]
    sooner = [(i, i) if (i, j) in later else (i, j) for i, j in beyond]

    def halo(outer, inner, again):
        from_inner = lax.ppermute(inner, "lon", within)
        from_later = lax.ppermute(again, "lon", later)
        return lax.ppermute(outer, "lon", sooner), from_inner, from_later

    def misfit_halo(outer, inner):
        from_inner = lax.ppermute(inner, "lon", within)
        return lax.ppermute(outer, ("mem", "lon"), across), from_inner

    control = control.reshape(MEMBERS, OWN, LAT)
    perturb = perturb.reshape(MEMBERS, OWN, LAT)
    square = OWN * LAT
    matmul = 2 * OWN * LAT * LAT
    quarter = OWN // XS

    c_outer, c_inner, c_later = halo(
        *call(
            pack_kernel, (half_like(MEMBERS),) * 3, (control,), [HBM], 0, 8 * square,
            (pltpu.VMEM((MEMBERS, OWN, LAT), BF), pltpu.SemaphoreType.DMA((MEMBERS * PACK_PARTS,))),
        )
    )
    (
        side, back_own, back_side, partial, p_outer, p_inner, lat, control, weighted, scale, prec,
        innov,
    ) = call(
        first_kernel,
        (
            jax.ShapeDtypeStruct((OWN, 2 * SIDE), BF),
            jax.ShapeDtypeStruct((OWN, OWN), BF),
            jax.ShapeDtypeStruct((OWN, 2 * SIDE), BF),
            jax.ShapeDtypeStruct((OWN, LAT), F32),
            half_like(MEMBERS),
            half_like(MEMBERS),
            jax.ShapeDtypeStruct(lat_inverse.shape, BF),
            jax.ShapeDtypeStruct(control.shape, BF),
            jax.ShapeDtypeStruct(perturb.shape, F32),
            jax.ShapeDtypeStruct((MEMBERS, ROWS, LAT), F32),
            jax.ShapeDtypeStruct((quarter, LAT), BF),
            jax.ShapeDtypeStruct((quarter, LAT), BF),
        ),
        (member_group, group_weight, step_counts, step_counts.reshape(1, LEV), vert_inverse,
         lat_inverse, control, perturb, precision.reshape(OWN, LAT), innovation.reshape(OWN, LAT)),
        [HBM] * 10,
        4 * matmul, 20 * square,
        (
            pltpu.VMEM((KMAX, ROWS, OWN), F32),
            pltpu.SMEM(member_group.shape, jnp.int32),
            pltpu.SMEM(group_weight.shape, F32),
            pltpu.SMEM(step_counts.shape, jnp.int32),
            pltpu.VMEM((1, LEV), jnp.int32),
            pltpu.VMEM(vert_inverse.shape, F32),
            pltpu.VMEM(perturb.shape, BF),
            pltpu.SemaphoreType.DMA((10,)),
        ),
    )
    partial = call(
        functools.partial(forward_kernel, lons),
        jax.ShapeDtypeStruct((OWN, LAT), BF),
        (side, lat, c_outer, c_inner, c_later, weighted, partial),
        [VMEM] * 7,
        4 * matmul, 18 * square,
    )

    parts = lax.all_to_all(
        partial.reshape(XS, quarter, LAT), "mem", 0, 0, axis_index_groups=along_x
    )
    some = call(
        sum_kernel, jax.ShapeDtypeStruct((quarter, LAT), BF), (parts,), [VMEM], 0, 2 * square
    )
    some, p_inner, p_outer = lax.optimization_barrier((some, p_inner, p_outer))
    other = lax.ppermute(some, "mem", across_y)
    p_outer = lax.ppermute(p_outer, "lon", beyond)
    p_inner = lax.ppermute(p_inner, "lon", within)
    misfit = call(
        misfit_kernel,
        jax.ShapeDtypeStruct((XS, quarter, LAT), BF),
        (some, other, prec, innov),
        [VMEM] * 4,
        0, 2 * square,
    )
    misfit = lax.all_to_all(misfit, "mem", 0, 0, axis_index_groups=along_x).reshape(OWN, LAT)

    edge = jax.ShapeDtypeStruct((SIDE, LAT), BF)
    m_outer, m_inner = call(edge_kernel, (edge, edge), (misfit,), [VMEM], 0, 4 * square)
    m_inner, p_outer, p_inner = lax.optimization_barrier((m_inner, p_outer, p_inner))
    m_outer, m_inner = misfit_halo(m_outer, m_inner)
    base = call(
        back_own_kernel,
        jax.ShapeDtypeStruct((MEMBERS, OWN, LAT), F32),
        (back_own, lat, misfit, weighted, control),
        [VMEM] * 5,
        4 * matmul, 18 * square,
    )
    out = pl.pallas_call(
        back_side_kernel,
        out_shape=jax.ShapeDtypeStruct((MEMBERS, OWN, LAT), BF),
        in_specs=[VMEM] * 8,
        out_specs=HBM,
        scratch_shapes=(
            pltpu.VMEM((MEMBERS, OWN, LAT), BF),
            pltpu.SemaphoreType.DMA((2 * MEMBERS,)),
        ),
        compiler_params=pltpu.CompilerParams(vmem_limit_bytes=VMEM_LIMIT),
        cost_estimate=pl.CostEstimate(
            flops=4 * matmul, bytes_accessed=20 * square, transcendentals=0
        ),
    )(back_side, lat, m_outer, m_inner, p_outer, p_inner, scale, base)
    return out.reshape(MEMBERS, LEV, ROWS, LAT)


def solution(mesh):
    return jax.shard_map(
        shards,
        mesh=mesh,
        in_specs=(
            P("mem", None, "lon", None),
            P("mem", None, "lon", None),
            P("mem"),
            P(),
            P(),
            P(),
            P(),
            P(None, "lon", None),
            P(None, "lon", None),
        ),
        out_specs=P("mem", None, "lon", None),
        check_vma=False,
    )
```

```python
import functools

import jax
import jax.numpy as jnp
from jax import lax
from jax.experimental import pallas as pl
from jax.experimental.pallas import tpu as pltpu
from jax.sharding import PartitionSpec as P

LEV = 64
ROWS = 8
LAT = 512
KMAX = 4
HALO = 4
MEMBERS = 2
XS = 4
YS = 4
PACK_PARTS = 2
OWN = LEV * ROWS
SIDE = LEV * HALO

VMEM_LIMIT = 16 * 2**20

BF = jnp.bfloat16
F32 = jnp.float32
VMEM = pl.BlockSpec(memory_space=pltpu.VMEM)
HBM = pl.BlockSpec(memory_space=pltpu.HBM)

BAND = {
    1: {1: 0.5},
    2: {0: 0.5, 2: 0.25},
    3: {1: 0.375, 3: 0.125},
    4: {0: 0.375, 2: 0.25, 4: 0.0625},
}


def in_hbm(x):
    return pltpu.with_memory_space_constraint(x, pltpu.HBM)


def call(kernel, out, operands, specs, flops, moved, scratch=()):
    return pl.pallas_call(
        kernel,
        out_shape=out,
        in_specs=specs,
        out_specs=jax.tree.map(lambda _: VMEM, out),
        scratch_shapes=scratch,
        compiler_params=pltpu.CompilerParams(vmem_limit_bytes=VMEM_LIMIT),
        cost_estimate=pl.CostEstimate(flops=flops, bytes_accessed=moved, transcendentals=0),
    )(*(in_hbm(x) if spec is HBM else x for x, spec in zip(operands, specs)))


def halves(x):
    rows, columns = x.shape
    x = x.reshape(rows // (2 * ROWS), 2, ROWS, columns)
    even, odd = x[:, 0], x[:, 1]
    low = lax.broadcasted_iota(jnp.int32, even.shape, 1) < HALO
    top = jnp.where(low, even, pltpu.roll(odd, HALO, 1))
    bottom = jnp.where(low, pltpu.roll(even, HALO, 1), odd)
    return top.reshape(rows // 2, columns), bottom.reshape(rows // 2, columns)


def waits(lons):
    lon = lax.axis_index("lon")
    return (lon > lons - 2 * YS) & (lon < lons - 1)


def odd_place():
    return lax.rem(lax.axis_index("lon"), 2) == 1


def pack_into(odd, x, outer_ref, inner_ref, at):
    top, bottom = halves(x.astype(F32))
    outer_ref[at] = jnp.where(odd, bottom, top).astype(BF)
    inner_ref[at] = jnp.where(odd, top, bottom).astype(BF)


def pack_kernel(x_ref, outer_ref, inner_ref, again_ref, x, sems):
    odd = odd_place()
    part = OWN // PACK_PARTS
    copies = []
    for i in range(MEMBERS * PACK_PARTS):
        rows = (i // PACK_PARTS, pl.ds(i % PACK_PARTS * part, part))
        copies.append(pltpu.make_async_copy(x_ref.at[rows], x.at[rows], sems.at[i]))
        copies[-1].start()
    for i, copy in enumerate(copies):
        copy.wait()
        m, p = i // PACK_PARTS, i % PACK_PARTS
        at = (m, pl.ds(p * part // 2, part // 2))
        pack_into(odd, x[m, pl.ds(p * part, part)], outer_ref, inner_ref, at)
        again_ref[at] = outer_ref[at]


def half_like(members):
    return jax.ShapeDtypeStruct((members, SIDE, LAT), BF)


def weights(n, distance):
    total = jnp.zeros(distance.shape, F32)
    for sweeps, band in BAND.items():
        row = jnp.zeros(distance.shape, F32)
        for d, c in band.items():
            row = jnp.where(jnp.abs(distance) == d, jnp.float32(c), row)
        total = jnp.where(n == sweeps, row, total)
    return total


def spread_lanes(width, per):
    level = lax.broadcasted_iota(jnp.int32, (LEV, width), 0)
    lane = lax.broadcasted_iota(jnp.int32, (LEV, width), 1)
    return jnp.where(level == lane // per, F32(1.0), F32(0.0)).astype(BF)


def side_distance(odd):
    row = lax.broadcasted_iota(jnp.int32, (ROWS, 2 * SIDE), 0)
    lane = lax.broadcasted_iota(jnp.int32, (ROWS, 2 * SIDE), 1)
    left = (lane < SIDE) != odd
    place = jnp.where(left, lane % HALO - HALO, lane % HALO + ROWS)
    return place - row


def own_distance():
    row = lax.broadcasted_iota(jnp.int32, (ROWS, OWN), 0)
    lane = lax.broadcasted_iota(jnp.int32, (ROWS, OWN), 1)
    return lane % ROWS - row


def first_kernel(
    group_hbm, weight_hbm, steps_hbm, steps_row_hbm, vert_hbm, lat_hbm, control_hbm, perturb_hbm,
    precision_hbm, innovation_hbm,
    side_ref, back_own_ref, back_side_ref, partial_ref, p_outer_ref, p_inner_ref,
    lat_ref, control_ref, weighted_ref, scale_ref, precision_ref, innovation_ref,
    table, group_ref, weight_ref, steps_ref, steps_row_ref, vert_ref, perturb_ref, sems,
):
    odd = odd_place()
    quarter = precision_ref.shape[0]
    start = pl.multiple_of(lax.rem(lax.axis_index("mem"), XS) * quarter, quarter)
    moves = [
        (vert_hbm, vert_ref),
        (steps_row_hbm, steps_row_ref),
        (steps_hbm, steps_ref),
        (group_hbm, group_ref),
        (weight_hbm, weight_ref),
        (control_hbm, control_ref),
        (lat_hbm, lat_ref),
        (perturb_hbm, perturb_ref),
        (precision_hbm.at[pl.ds(start, quarter)], precision_ref),
        (innovation_hbm.at[pl.ds(start, quarter)], innovation_ref),
    ]
    copies = [pltpu.make_async_copy(a, b, sems.at[i]) for i, (a, b) in enumerate(moves)]
    for copy in copies:
        copy.start()
    for copy in copies[:5]:
        copy.wait()

    vert = vert_ref[...].astype(BF)
    steps_row = steps_row_ref[...].astype(F32).astype(BF)
    lanes_own = spread_lanes(OWN, ROWS)
    lanes_half = spread_lanes(SIDE, HALO)
    lanes_side = jnp.concatenate([lanes_half, lanes_half], axis=1)

    def expand(matrix, lanes, dims=(((1,), (0,)), ((), ()))):
        return lax.dot_general(matrix, lanes, dims, preferred_element_type=F32)

    def forward(lanes, distance):
        n = expand(steps_row, lanes)
        wide = expand(vert, lanes)
        band = weights(n, distance)
        return (wide[:, None, :] * band[None]).reshape(OWN, OWN).astype(BF)

    side_ref[...] = forward(lanes_side, side_distance(odd))
    own = forward(lanes_own, own_distance())

    first_dim = (((0,), (0,)), ((), ()))
    for lanes, distance, out_ref in (
        (lanes_own, own_distance(), back_own_ref),
        (lanes_side, side_distance(odd), back_side_ref),
    ):
        wide = expand(vert, lanes, first_dim)
        for n in range(1, KMAX + 1):
            table[n - 1] = weights(n, distance)
        for l in range(0, LEV, 2):
            pair = [wide[l + i : l + i + 1] * table[steps_ref[l + i] - 1] for i in range(2)]
            out_ref[pl.ds(l * ROWS, 2 * ROWS), :] = jnp.concatenate(pair, axis=0).astype(BF)

    for copy in copies[5:]:
        copy.wait()
    total = jnp.zeros((OWN, LAT), F32)
    for m in range(MEMBERS):
        pack_into(odd, perturb_ref[m], p_outer_ref, p_inner_ref, m)
        weight = weight_ref[group_ref[m]]
        scale_ref[m] = jnp.full((ROWS, LAT), weight)
        weighted = weight * perturb_ref[m].astype(F32)
        weighted_ref[m] = weighted
        mixed = jnp.dot(own, control_ref[m], preferred_element_type=F32).astype(BF)
        total += weighted * jnp.dot(mixed, lat_ref[...], preferred_element_type=F32)
    partial_ref[...] = total


def forward_kernel(
    lons, side_ref, lat_ref, outer_ref, inner_ref, later_ref, weighted_ref, partial_ref, out_ref
):
    late = waits(lons)
    total = partial_ref[...]
    for m in range(MEMBERS):
        outer = jnp.where(late, later_ref[m], outer_ref[m])
        mixed = jnp.dot(side_ref[:, :SIDE], outer, preferred_element_type=F32)
        mixed += jnp.dot(side_ref[:, SIDE:], inner_ref[m], preferred_element_type=F32)
        local = jnp.dot(mixed.astype(BF), lat_ref[...], preferred_element_type=F32)
        total += weighted_ref[m] * local
    out_ref[...] = total.astype(BF)


def misfit_kernel(some_ref, other_ref, precision_ref, innovation_ref, out_ref):
    increment = some_ref[...].astype(F32) + other_ref[...].astype(F32)
    departure = increment - innovation_ref[...].astype(F32)
    misfit = (precision_ref[...].astype(F32) * departure).astype(BF)
    for j in range(XS):
        out_ref[j] = misfit


def edge_kernel(misfit_ref, outer_ref, inner_ref):
    pack_into(odd_place(), misfit_ref[...], outer_ref, inner_ref, ...)


def sum_kernel(parts_ref, out_ref):
    out_ref[...] = jnp.sum(parts_ref[...].astype(F32), axis=0).astype(BF)


LAST = (((1,), (1,)), ((), ()))


def back_own_kernel(back_own_ref, lat_ref, misfit_ref, weighted_ref, control_ref, out_ref):
    misfit = misfit_ref[...].astype(F32)
    for m in range(MEMBERS):
        back = (weighted_ref[m] * misfit).astype(BF)
        mixed = jnp.dot(back_own_ref[...], back, preferred_element_type=F32).astype(BF)
        latback = lax.dot_general(mixed, lat_ref[...], LAST, preferred_element_type=F32)
        out_ref[m] = control_ref[m].astype(F32) + latback


def back_side_kernel(
    back_side_ref, lat_ref, outer_ref, inner_ref, p_outer_ref, p_inner_ref, scale_ref, base_ref,
    out_hbm, out, sems,
):
    def back(m, p_ref, misfit_ref):
        p = p_ref[m].astype(F32).reshape(SIDE // ROWS, ROWS, LAT)
        weighted = (scale_ref[m][None] * p).reshape(SIDE, LAT)
        return (weighted * misfit_ref[...].astype(F32)).astype(BF)

    copies = []
    for m in range(MEMBERS):
        from_outer = back(m, p_outer_ref, outer_ref)
        from_inner = back(m, p_inner_ref, inner_ref)
        sides = jnp.concatenate([from_outer, from_inner], axis=0)
        mixed = jnp.dot(back_side_ref[...], sides, preferred_element_type=F32).astype(BF)
        latback = lax.dot_general(mixed, lat_ref[...], LAST, preferred_element_type=F32)
        out[m] = (base_ref[m] + latback).astype(BF)
        copies.append(pltpu.make_async_copy(out.at[m], out_hbm.at[m], sems.at[m]))
        copies[m].start()
    for copy in copies:
        copy.wait()


def shards(
    control,
    perturb,
    member_group,
    group_weight,
    step_counts,
    lat_inverse,
    vert_inverse,
    innovation,
    precision,
):
    lons = lax.axis_size("lon")
    within = [(i, i + 1 - 2 * (i % 2)) for i in range(lons)]
    beyond = [(i, (i - 1 + 2 * (i % 2)) % lons) for i in range(lons)]
    mems = lax.axis_size("mem")
    along_x = [list(range(i, i + XS)) for i in range(0, mems, XS)]
    across_y = [(i, (i + XS) % mems) for i in range(mems)]

    run = 2 * YS
    across = [
        (m * lons + i, (m if i // run == j // run else (m + XS) % mems) * lons + j)
        for m in range(mems)
        for i, j in beyond
    ]

    later = [(i, j) for i, j in beyond if lons - run < i < lons - 1]
    sooner = [(i, i) if (i, j) in later else (i, j) for i, j in beyond]

    def halo(outer, inner, again):
        from_inner = lax.ppermute(inner, "lon", within)
        from_later = lax.ppermute(again, "lon", later)
        return lax.ppermute(outer, "lon", sooner), from_inner, from_later

    def misfit_halo(outer, inner):
        from_inner = lax.ppermute(inner, "lon", within)
        return lax.ppermute(outer, ("mem", "lon"), across), from_inner

    control = control.reshape(MEMBERS, OWN, LAT)
    perturb = perturb.reshape(MEMBERS, OWN, LAT)
    square = OWN * LAT
    matmul = 2 * OWN * LAT * LAT
    quarter = OWN // XS

    c_outer, c_inner, c_later = halo(
        *call(
            pack_kernel, (half_like(MEMBERS),) * 3, (control,), [HBM], 0, 8 * square,
            (pltpu.VMEM((MEMBERS, OWN, LAT), BF), pltpu.SemaphoreType.DMA((MEMBERS * PACK_PARTS,))),
        )
    )
    (
        side, back_own, back_side, partial, p_outer, p_inner, lat, control, weighted, scale, prec,
        innov,
    ) = call(
        first_kernel,
        (
            jax.ShapeDtypeStruct((OWN, 2 * SIDE), BF),
            jax.ShapeDtypeStruct((OWN, OWN), BF),
            jax.ShapeDtypeStruct((OWN, 2 * SIDE), BF),
            jax.ShapeDtypeStruct((OWN, LAT), F32),
            half_like(MEMBERS),
            half_like(MEMBERS),
            jax.ShapeDtypeStruct(lat_inverse.shape, BF),
            jax.ShapeDtypeStruct(control.shape, BF),
            jax.ShapeDtypeStruct(perturb.shape, F32),
            jax.ShapeDtypeStruct((MEMBERS, ROWS, LAT), F32),
            jax.ShapeDtypeStruct((quarter, LAT), BF),
            jax.ShapeDtypeStruct((quarter, LAT), BF),
        ),
        (member_group, group_weight, step_counts, step_counts.reshape(1, LEV), vert_inverse,
         lat_inverse, control, perturb, precision.reshape(OWN, LAT), innovation.reshape(OWN, LAT)),
        [HBM] * 10,
        4 * matmul, 20 * square,
        (
            pltpu.VMEM((KMAX, ROWS, OWN), F32),
            pltpu.SMEM(member_group.shape, jnp.int32),
            pltpu.SMEM(group_weight.shape, F32),
            pltpu.SMEM(step_counts.shape, jnp.int32),
            pltpu.VMEM((1, LEV), jnp.int32),
            pltpu.VMEM(vert_inverse.shape, F32),
            pltpu.VMEM(perturb.shape, BF),
            pltpu.SemaphoreType.DMA((10,)),
        ),
    )
    partial = call(
        functools.partial(forward_kernel, lons),
        jax.ShapeDtypeStruct((OWN, LAT), BF),
        (side, lat, c_outer, c_inner, c_later, weighted, partial),
        [VMEM] * 7,
        4 * matmul, 18 * square,
    )

    parts = lax.all_to_all(
        partial.reshape(XS, quarter, LAT), "mem", 0, 0, axis_index_groups=along_x
    )
    some = call(
        sum_kernel, jax.ShapeDtypeStruct((quarter, LAT), BF), (parts,), [VMEM], 0, 2 * square
    )
    some, p_inner, p_outer = lax.optimization_barrier((some, p_inner, p_outer))
    other = lax.ppermute(some, "mem", across_y)
    p_outer = lax.ppermute(p_outer, "lon", beyond)
    p_inner = lax.ppermute(p_inner, "lon", within)
    misfit = call(
        misfit_kernel,
        jax.ShapeDtypeStruct((XS, quarter, LAT), BF),
        (some, other, prec, innov),
        [VMEM] * 4,
        0, 2 * square,
    )
    misfit = lax.all_to_all(misfit, "mem", 0, 0, axis_index_groups=along_x).reshape(OWN, LAT)

    edge = jax.ShapeDtypeStruct((SIDE, LAT), BF)
    m_outer, m_inner = call(edge_kernel, (edge, edge), (misfit,), [VMEM], 0, 4 * square)
    m_inner, p_outer, p_inner = lax.optimization_barrier((m_inner, p_outer, p_inner))
    m_outer, m_inner = misfit_halo(m_outer, m_inner)
    base = call(
        back_own_kernel,
        jax.ShapeDtypeStruct((MEMBERS, OWN, LAT), F32),
        (back_own, lat, misfit, weighted, control),
        [VMEM] * 5,
        4 * matmul, 18 * square,
    )
    out = pl.pallas_call(
        back_side_kernel,
        out_shape=jax.ShapeDtypeStruct((MEMBERS, OWN, LAT), BF),
        in_specs=[VMEM] * 8,
        out_specs=HBM,
        scratch_shapes=(
            pltpu.VMEM((MEMBERS, OWN, LAT), BF),
            pltpu.SemaphoreType.DMA((MEMBERS,)),
        ),
        compiler_params=pltpu.CompilerParams(vmem_limit_bytes=VMEM_LIMIT),
        cost_estimate=pl.CostEstimate(
            flops=4 * matmul, bytes_accessed=20 * square, transcendentals=0
        ),
    )(back_side, lat, m_outer, m_inner, p_outer, p_inner, scale, base)
    return out.reshape(MEMBERS, LEV, ROWS, LAT)


def solution(mesh):
    return jax.shard_map(
        shards,
        mesh=mesh,
        in_specs=(
            P("mem", None, "lon", None),
            P("mem", None, "lon", None),
            P("mem"),
            P(),
            P(),
            P(),
            P(),
            P(None, "lon", None),
            P(None, "lon", None),
        ),
        out_specs=P("mem", None, "lon", None),
        check_vma=False,
    )
```

```python
import functools

import jax
import jax.numpy as jnp
from jax import lax
from jax.experimental import pallas as pl
from jax.experimental.pallas import tpu as pltpu
from jax.sharding import PartitionSpec as P

LEV = 64
ROWS = 8
LAT = 512
KMAX = 4
HALO = 4
MEMBERS = 2
XS = 4
YS = 4
PACK_PARTS = 2
OWN = LEV * ROWS
SIDE = LEV * HALO

VMEM_LIMIT = 16 * 2**20

BF = jnp.bfloat16
F32 = jnp.float32
VMEM = pl.BlockSpec(memory_space=pltpu.VMEM)
HBM = pl.BlockSpec(memory_space=pltpu.HBM)

BAND = {
    1: {1: 0.5},
    2: {0: 0.5, 2: 0.25},
    3: {1: 0.375, 3: 0.125},
    4: {0: 0.375, 2: 0.25, 4: 0.0625},
}


def in_hbm(x):
    return pltpu.with_memory_space_constraint(x, pltpu.HBM)


def call(kernel, out, operands, specs, flops, moved, scratch=()):
    return pl.pallas_call(
        kernel,
        out_shape=out,
        in_specs=specs,
        out_specs=jax.tree.map(lambda _: VMEM, out),
        scratch_shapes=scratch,
        compiler_params=pltpu.CompilerParams(vmem_limit_bytes=VMEM_LIMIT),
        cost_estimate=pl.CostEstimate(flops=flops, bytes_accessed=moved, transcendentals=0),
    )(*(in_hbm(x) if spec is HBM else x for x, spec in zip(operands, specs)))


def halves(x):
    rows, columns = x.shape
    x = x.reshape(rows // (2 * ROWS), 2, ROWS, columns)
    even, odd = x[:, 0], x[:, 1]
    low = lax.broadcasted_iota(jnp.int32, even.shape, 1) < HALO
    top = jnp.where(low, even, pltpu.roll(odd, HALO, 1))
    bottom = jnp.where(low, pltpu.roll(even, HALO, 1), odd)
    return top.reshape(rows // 2, columns), bottom.reshape(rows // 2, columns)


def waits(lons):
    lon = lax.axis_index("lon")
    return (lon > lons - 2 * YS) & (lon < lons - 1)


def odd_place():
    return lax.rem(lax.axis_index("lon"), 2) == 1


def pack_into(odd, x, outer_ref, inner_ref, at):
    top, bottom = halves(x.astype(F32))
    outer_ref[at] = jnp.where(odd, bottom, top).astype(BF)
    inner_ref[at] = jnp.where(odd, top, bottom).astype(BF)


def pack_kernel(lons, x_ref, outer_ref, inner_ref, again_ref, x, sems):
    odd = odd_place()
    part = OWN // PACK_PARTS
    copies = []
    for i in range(MEMBERS * PACK_PARTS):
        rows = (i // PACK_PARTS, pl.ds(i % PACK_PARTS * part, part))
        copies.append(pltpu.make_async_copy(x_ref.at[rows], x.at[rows], sems.at[i]))
        copies[-1].start()
    for i, copy in enumerate(copies):
        copy.wait()
        m, p = i // PACK_PARTS, i % PACK_PARTS
        at = (m, pl.ds(p * part // 2, part // 2))
        pack_into(odd, x[m, pl.ds(p * part, part)], outer_ref, inner_ref, at)

    @pl.when(waits(lons))
    def _():
        again_ref[...] = outer_ref[...]


def half_like(members):
    return jax.ShapeDtypeStruct((members, SIDE, LAT), BF)


def weights(n, distance):
    total = jnp.zeros(distance.shape, F32)
    for sweeps, band in BAND.items():
        row = jnp.zeros(distance.shape, F32)
        for d, c in band.items():
            row = jnp.where(jnp.abs(distance) == d, jnp.float32(c), row)
        total = jnp.where(n == sweeps, row, total)
    return total


def spread_lanes(width, per):
    level = lax.broadcasted_iota(jnp.int32, (LEV, width), 0)
    lane = lax.broadcasted_iota(jnp.int32, (LEV, width), 1)
    return jnp.where(level == lane // per, F32(1.0), F32(0.0)).astype(BF)


def side_distance(odd):
    row = lax.broadcasted_iota(jnp.int32, (ROWS, 2 * SIDE), 0)
    lane = lax.broadcasted_iota(jnp.int32, (ROWS, 2 * SIDE), 1)
    left = (lane < SIDE) != odd
    place = jnp.where(left, lane % HALO - HALO, lane % HALO + ROWS)
    return place - row


def own_distance():
    row = lax.broadcasted_iota(jnp.int32, (ROWS, OWN), 0)
    lane = lax.broadcasted_iota(jnp.int32, (ROWS, OWN), 1)
    return lane % ROWS - row


def first_kernel(
    group_hbm, weight_hbm, steps_hbm, steps_row_hbm, vert_hbm, lat_hbm, control_hbm, perturb_hbm,
    precision_hbm, innovation_hbm,
    side_ref, back_own_ref, back_side_ref, partial_ref, p_outer_ref, p_inner_ref,
    lat_ref, control_ref, weighted_ref, scale_ref, precision_ref, innovation_ref,
    table, group_ref, weight_ref, steps_ref, steps_row_ref, vert_ref, perturb_ref, sems,
):
    odd = odd_place()
    quarter = precision_ref.shape[0]
    start = pl.multiple_of(lax.rem(lax.axis_index("mem"), XS) * quarter, quarter)
    moves = [
        (vert_hbm, vert_ref),
        (steps_row_hbm, steps_row_ref),
        (steps_hbm, steps_ref),
        (group_hbm, group_ref),
        (weight_hbm, weight_ref),
        (control_hbm, control_ref),
        (lat_hbm, lat_ref),
        (perturb_hbm, perturb_ref),
        (precision_hbm.at[pl.ds(start, quarter)], precision_ref),
        (innovation_hbm.at[pl.ds(start, quarter)], innovation_ref),
    ]
    copies = [pltpu.make_async_copy(a, b, sems.at[i]) for i, (a, b) in enumerate(moves)]
    for copy in copies:
        copy.start()
    for copy in copies[:5]:
        copy.wait()

    vert = vert_ref[...].astype(BF)
    steps_row = steps_row_ref[...].astype(F32).astype(BF)
    lanes_own = spread_lanes(OWN, ROWS)
    lanes_half = spread_lanes(SIDE, HALO)
    lanes_side = jnp.concatenate([lanes_half, lanes_half], axis=1)

    def expand(matrix, lanes, dims=(((1,), (0,)), ((), ()))):
        return lax.dot_general(matrix, lanes, dims, preferred_element_type=F32)

    def forward(lanes, distance):
        n = expand(steps_row, lanes)
        wide = expand(vert, lanes)
        band = weights(n, distance)
        return (wide[:, None, :] * band[None]).reshape(OWN, OWN).astype(BF)

    side_ref[...] = forward(lanes_side, side_distance(odd))
    own = forward(lanes_own, own_distance())

    first_dim = (((0,), (0,)), ((), ()))
    for lanes, distance, out_ref in (
        (lanes_own, own_distance(), back_own_ref),
        (lanes_side, side_distance(odd), back_side_ref),
    ):
        wide = expand(vert, lanes, first_dim)
        for n in range(1, KMAX + 1):
            table[n - 1] = weights(n, distance)
        for l in range(0, LEV, 2):
            pair = [wide[l + i : l + i + 1] * table[steps_ref[l + i] - 1] for i in range(2)]
            out_ref[pl.ds(l * ROWS, 2 * ROWS), :] = jnp.concatenate(pair, axis=0).astype(BF)

    for copy in copies[5:]:
        copy.wait()
    total = jnp.zeros((OWN, LAT), F32)
    for m in range(MEMBERS):
        pack_into(odd, perturb_ref[m], p_outer_ref, p_inner_ref, m)
        weight = weight_ref[group_ref[m]]
        scale_ref[m] = jnp.full((ROWS, LAT), weight)
        weighted = weight * perturb_ref[m].astype(F32)
        weighted_ref[m] = weighted
        mixed = jnp.dot(own, control_ref[m], preferred_element_type=F32).astype(BF)
        total += weighted * jnp.dot(mixed, lat_ref[...], preferred_element_type=F32)
    partial_ref[...] = total


def forward_kernel(
    lons, side_ref, lat_ref, outer_ref, inner_ref, later_ref, weighted_ref, partial_ref, out_ref
):
    late = waits(lons)
    total = partial_ref[...]
    for m in range(MEMBERS):
        outer = jnp.where(late, later_ref[m], outer_ref[m])
        mixed = jnp.dot(side_ref[:, :SIDE], outer, preferred_element_type=F32)
        mixed += jnp.dot(side_ref[:, SIDE:], inner_ref[m], preferred_element_type=F32)
        local = jnp.dot(mixed.astype(BF), lat_ref[...], preferred_element_type=F32)
        total += weighted_ref[m] * local
    out_ref[...] = total.astype(BF)


def misfit_kernel(some_ref, other_ref, precision_ref, innovation_ref, out_ref):
    increment = some_ref[...].astype(F32) + other_ref[...].astype(F32)
    departure = increment - innovation_ref[...].astype(F32)
    misfit = (precision_ref[...].astype(F32) * departure).astype(BF)
    for j in range(XS):
        out_ref[j] = misfit


def edge_kernel(misfit_ref, outer_ref, inner_ref):
    pack_into(odd_place(), misfit_ref[...], outer_ref, inner_ref, ...)


def sum_kernel(parts_ref, out_ref):
    out_ref[...] = jnp.sum(parts_ref[...].astype(F32), axis=0).astype(BF)


LAST = (((1,), (1,)), ((), ()))


def back_own_kernel(back_own_ref, lat_ref, misfit_ref, weighted_ref, control_ref, out_ref):
    misfit = misfit_ref[...].astype(F32)
    for m in range(MEMBERS):
        back = (weighted_ref[m] * misfit).astype(BF)
        mixed = jnp.dot(back_own_ref[...], back, preferred_element_type=F32).astype(BF)
        latback = lax.dot_general(mixed, lat_ref[...], LAST, preferred_element_type=F32)
        out_ref[m] = control_ref[m].astype(F32) + latback


def back_side_kernel(
    back_side_ref, lat_ref, outer_ref, inner_ref, p_outer_ref, p_inner_ref, scale_ref, base_ref,
    out_hbm, out, sems,
):
    def back(m, p_ref, misfit_ref):
        p = p_ref[m].astype(F32).reshape(SIDE // ROWS, ROWS, LAT)
        weighted = (scale_ref[m][None] * p).reshape(SIDE, LAT)
        return (weighted * misfit_ref[...].astype(F32)).astype(BF)

    copies = []
    for m in range(MEMBERS):
        from_outer = back(m, p_outer_ref, outer_ref)
        from_inner = back(m, p_inner_ref, inner_ref)
        sides = jnp.concatenate([from_outer, from_inner], axis=0)
        mixed = jnp.dot(back_side_ref[...], sides, preferred_element_type=F32).astype(BF)
        pieces = 1 if m < MEMBERS - 1 else 2
        width = LAT // pieces
        for h in range(pieces):
            columns = pl.ds(h * width, width)
            latback = lax.dot_general(mixed, lat_ref[columns, :], LAST, preferred_element_type=F32)
            out[m, :, columns] = (base_ref[m, :, columns] + latback).astype(BF)
            copy = pltpu.make_async_copy(
                out.at[m, :, columns], out_hbm.at[m, :, columns], sems.at[m + h]
            )
            copy.start()
            copies.append(copy)
    for copy in copies:
        copy.wait()


def shards(
    control,
    perturb,
    member_group,
    group_weight,
    step_counts,
    lat_inverse,
    vert_inverse,
    innovation,
    precision,
):
    lons = lax.axis_size("lon")
    within = [(i, i + 1 - 2 * (i % 2)) for i in range(lons)]
    beyond = [(i, (i - 1 + 2 * (i % 2)) % lons) for i in range(lons)]
    mems = lax.axis_size("mem")
    along_x = [list(range(i, i + XS)) for i in range(0, mems, XS)]
    across_y = [(i, (i + XS) % mems) for i in range(mems)]

    run = 2 * YS
    across = [
        (m * lons + i, (m if i // run == j // run else (m + XS) % mems) * lons + j)
        for m in range(mems)
        for i, j in beyond
    ]

    later = [(i, j) for i, j in beyond if lons - run < i < lons - 1]
    sooner = [(i, i) if (i, j) in later else (i, j) for i, j in beyond]

    def halo(outer, inner, again):
        from_inner = lax.ppermute(inner, "lon", within)
        from_later = lax.ppermute(again, "lon", later)
        return lax.ppermute(outer, "lon", sooner), from_inner, from_later

    def misfit_halo(outer, inner):
        from_inner = lax.ppermute(inner, "lon", within)
        return lax.ppermute(outer, ("mem", "lon"), across), from_inner

    control = control.reshape(MEMBERS, OWN, LAT)
    perturb = perturb.reshape(MEMBERS, OWN, LAT)
    square = OWN * LAT
    matmul = 2 * OWN * LAT * LAT
    quarter = OWN // XS

    c_outer, c_inner, c_later = halo(
        *call(
            functools.partial(pack_kernel, lons), (half_like(MEMBERS),) * 3, (control,), [HBM], 0, 8 * square,
            (pltpu.VMEM((MEMBERS, OWN, LAT), BF), pltpu.SemaphoreType.DMA((MEMBERS * PACK_PARTS,))),
        )
    )
    (
        side, back_own, back_side, partial, p_outer, p_inner, lat, control, weighted, scale, prec,
        innov,
    ) = call(
        first_kernel,
        (
            jax.ShapeDtypeStruct((OWN, 2 * SIDE), BF),
            jax.ShapeDtypeStruct((OWN, OWN), BF),
            jax.ShapeDtypeStruct((OWN, 2 * SIDE), BF),
            jax.ShapeDtypeStruct((OWN, LAT), F32),
            half_like(MEMBERS),
            half_like(MEMBERS),
            jax.ShapeDtypeStruct(lat_inverse.shape, BF),
            jax.ShapeDtypeStruct(control.shape, BF),
            jax.ShapeDtypeStruct(perturb.shape, F32),
            jax.ShapeDtypeStruct((MEMBERS, ROWS, LAT), F32),
            jax.ShapeDtypeStruct((quarter, LAT), BF),
            jax.ShapeDtypeStruct((quarter, LAT), BF),
        ),
        (member_group, group_weight, step_counts, step_counts.reshape(1, LEV), vert_inverse,
         lat_inverse, control, perturb, precision.reshape(OWN, LAT), innovation.reshape(OWN, LAT)),
        [HBM] * 10,
        4 * matmul, 20 * square,
        (
            pltpu.VMEM((KMAX, ROWS, OWN), F32),
            pltpu.SMEM(member_group.shape, jnp.int32),
            pltpu.SMEM(group_weight.shape, F32),
            pltpu.SMEM(step_counts.shape, jnp.int32),
            pltpu.VMEM((1, LEV), jnp.int32),
            pltpu.VMEM(vert_inverse.shape, F32),
            pltpu.VMEM(perturb.shape, BF),
            pltpu.SemaphoreType.DMA((10,)),
        ),
    )
    partial = call(
        functools.partial(forward_kernel, lons),
        jax.ShapeDtypeStruct((OWN, LAT), BF),
        (side, lat, c_outer, c_inner, c_later, weighted, partial),
        [VMEM] * 7,
        4 * matmul, 18 * square,
    )

    parts = lax.all_to_all(
        partial.reshape(XS, quarter, LAT), "mem", 0, 0, axis_index_groups=along_x
    )
    some = call(
        sum_kernel, jax.ShapeDtypeStruct((quarter, LAT), BF), (parts,), [VMEM], 0, 2 * square
    )
    some, p_inner, p_outer = lax.optimization_barrier((some, p_inner, p_outer))
    other = lax.ppermute(some, "mem", across_y)
    p_outer = lax.ppermute(p_outer, "lon", beyond)
    p_inner = lax.ppermute(p_inner, "lon", within)
    misfit = call(
        misfit_kernel,
        jax.ShapeDtypeStruct((XS, quarter, LAT), BF),
        (some, other, prec, innov),
        [VMEM] * 4,
        0, 2 * square,
    )
    misfit = lax.all_to_all(misfit, "mem", 0, 0, axis_index_groups=along_x).reshape(OWN, LAT)

    edge = jax.ShapeDtypeStruct((SIDE, LAT), BF)
    m_outer, m_inner = call(edge_kernel, (edge, edge), (misfit,), [VMEM], 0, 4 * square)
    m_inner, p_outer, p_inner = lax.optimization_barrier((m_inner, p_outer, p_inner))
    m_outer, m_inner = misfit_halo(m_outer, m_inner)
    base = call(
        back_own_kernel,
        jax.ShapeDtypeStruct((MEMBERS, OWN, LAT), F32),
        (back_own, lat, misfit, weighted, control),
        [VMEM] * 5,
        4 * matmul, 18 * square,
    )
    out = pl.pallas_call(
        back_side_kernel,
        out_shape=jax.ShapeDtypeStruct((MEMBERS, OWN, LAT), BF),
        in_specs=[VMEM] * 8,
        out_specs=HBM,
        scratch_shapes=(
            pltpu.VMEM((MEMBERS, OWN, LAT), BF),
            pltpu.SemaphoreType.DMA((MEMBERS + 1,)),
        ),
        compiler_params=pltpu.CompilerParams(vmem_limit_bytes=VMEM_LIMIT),
        cost_estimate=pl.CostEstimate(
            flops=4 * matmul, bytes_accessed=20 * square, transcendentals=0
        ),
    )(back_side, lat, m_outer, m_inner, p_outer, p_inner, scale, base)
    return out.reshape(MEMBERS, LEV, ROWS, LAT)


def solution(mesh):
    return jax.shard_map(
        shards,
        mesh=mesh,
        in_specs=(
            P("mem", None, "lon", None),
            P("mem", None, "lon", None),
            P("mem"),
            P(),
            P(),
            P(),
            P(),
            P(None, "lon", None),
            P(None, "lon", None),
        ),
        out_specs=P("mem", None, "lon", None),
        check_vma=False,
    )
```
